256 devices in a mesh: rep: 64 (over z, y, x_hi), tp: 4 (over x_lo, core).
Axes of the slice: x: 4 (x_hi: 2, x_lo: 2; x = x_hi * 2 + x_lo), y: 4, z: 8, core: 2. Of those that a mesh axis runs over, the one named last changes fastest.
Arguments:
- momentum: bfloat16 [64, 128, 13824], P('rep', None, 'tp'), may hold values from -6 to 6
- grad: bfloat16 [64, 128, 13824], P('rep', None, 'tp'), may hold values from -64 to 64
- freq_rows: int32 [8], replicated, may hold values from 0 to 15, as said below
- freq_cols: int32 [8], replicated, may hold values from 0 to 15, as said below
Outputs:
- momentum_out: bfloat16 [64, 128, 13824], P('rep', None, 'tp')
- update: float32 [128, 13824], P(None, 'tp')
The draws below stay inside these ranges and needn't reach their ends.
Inputs may be any that keep to these rules, and one draw needn't show every extreme that they name: `freq_rows`: 8 distinct frequencies, among them 0 and 15. `freq_cols`: 8 distinct frequencies, among them 0 and 15.
All inputs are finite; a program needn't handle non-finite values.
Results may differ from the reference program's by a relative error of at most 0.001.
Values sent between devices are 32-bit elements; how exact they have to be, the bound alone decides.
No kernel may reach another device: no remote copies, remote signals or barrier semaphores. Data moves between devices by JAX's collectives and lax.ppermute only.
A program may use at most 64 MiB of HBM per device.

```python
import math
import jax
import jax.numpy as jnp
from jax import lax

BLOCK = 64
KEEP = 8
FF = 13824
ROWS = 128
REPLICAS = 64


def pick_freqs(key):
    first, second = jax.random.split(key)
    middle = 1 + jax.random.permutation(first, 2 * KEEP - 2)[:KEEP - 2]
    values = jnp.concatenate([jnp.array([0, 2 * KEEP - 1], dtype=jnp.int32), middle.astype(jnp.int32)])
    order = jax.random.permutation(second, KEEP)
    return values[order].astype(jnp.int32)


def draw_freq_rows(key, part):
    key = jax.random.fold_in(key, 11)
    return pick_freqs(key)


def draw_freq_cols(key, part):
    key = jax.random.fold_in(key, 23)
    return pick_freqs(key)


def draw_grad(key, part):
    key = jax.random.fold_in(key, 7)
    k_rows, k_cols, k_noise = jax.random.split(key, 3)
    row_scale = jnp.exp(jax.random.uniform(k_rows, (1, ROWS, 1), jnp.float32, 0.0, math.log(3.2)))
    ramp = 1.0 + 2.0 * jnp.arange(FF, dtype=jnp.float32) / (FF - 1)
    col_scale = jnp.exp(jax.random.uniform(k_cols, (1, 1, FF), jnp.float32, math.log(0.5), math.log(1.6))) * ramp
    base = jnp.clip(jax.random.normal(k_noise, (REPLICAS, ROWS, FF), jnp.float32), -4.0, 4.0)
    return (base * row_scale * col_scale).astype(jnp.bfloat16)


def shard_levels(key, extent, cuts, smallest, top_value):
    def one(position, blocks):
        heights = jax.random.uniform(jax.random.fold_in(jax.random.fold_in(key, 6), position), (blocks,), jnp.float32, smallest / len(cuts), top_value / len(cuts))
        return jnp.repeat(jnp.exp(heights), extent[position] // blocks).reshape((-1,) + (1,) * (len(extent) - position - 1))

    loudness = one(*cuts[0])
    for cut in cuts[1:]:
        loudness = loudness * one(*cut)
    return loudness


def scatter_about(key, dims, spread, limit, pieces=(), kind=jnp.bfloat16):
    values = jax.random.normal(key, dims, jnp.float32) * spread
    if len(pieces) > 0:
        values = shard_levels(key, dims, pieces, -0.22, 0.18) * values
    return jnp.clip(values, min=-limit, max=limit).astype(kind)


def setup_inputs(seed: int = 0) -> dict:
    streams_of = jax.random.split(jax.random.key(seed), 5)
    momentum = scatter_about(streams_of[0], (REPLICAS, ROWS, FF), 1.0, 6.0, ((0, 64), (2, 4)))
    grad = draw_grad(jax.random.fold_in(streams_of[4], 71), 0)
    freq_rows = draw_freq_rows(jax.random.fold_in(streams_of[4], 71), 0)
    freq_cols = draw_freq_cols(jax.random.fold_in(streams_of[4], 71), 0)
    return dict(momentum=momentum, grad=grad, freq_rows=freq_rows, freq_cols=freq_cols)


def basis(freqs):
    points = jnp.arange(BLOCK, dtype=jnp.float32)
    waves = freqs.astype(jnp.float32)[:, None]
    scale = jnp.where(freqs == 0, math.sqrt(1.0 / BLOCK), math.sqrt(2.0 / BLOCK)).astype(jnp.float32)
    return scale[:, None] * jnp.cos(math.pi * (2.0 * points[None, :] + 1.0) * waves / (2.0 * BLOCK))

def forward(fresh, row_basis, col_basis):
    nrows, ncols = fresh.shape
    blocks = fresh.reshape(nrows, ncols // BLOCK, BLOCK)
    right = jnp.einsum('rcq,jq->rcj', blocks, col_basis, precision=lax.Precision.HIGHEST)
    right = right.reshape(nrows // BLOCK, BLOCK, -1)
    return jnp.einsum('ip,bpx->bix', row_basis, right, precision=lax.Precision.HIGHEST)

def inverse(coeffs, row_basis, col_basis):
    left = jnp.einsum('ip,bix->bpx', row_basis, coeffs, precision=lax.Precision.HIGHEST)
    left = left.reshape(coeffs.shape[0] * BLOCK, -1, KEEP)
    image = jnp.einsum('rcj,jq->rcq', left, col_basis, precision=lax.Precision.HIGHEST)
    return image.reshape(coeffs.shape[0] * BLOCK, -1)

def reference(momentum, grad, freq_rows, freq_cols):
    row_basis = basis(freq_rows)
    col_basis = basis(freq_cols)

    def replica(pair):
        fresh = 0.9 * pair[0].astype(jnp.float32) + pair[1].astype(jnp.float32)
        coeffs = forward(fresh, row_basis, col_basis)
        kept = (fresh - inverse(coeffs, row_basis, col_basis)).astype(jnp.bfloat16)
        return (kept, coeffs)
    momentum_out, coeffs = lax.map(replica, (momentum, grad))
    total = lax.optimization_barrier(jnp.sum(coeffs, axis=0))
    field = inverse(total, row_basis, col_basis)
    update = field / jnp.sqrt(jnp.mean(field * field) + 1e-06)
    return (momentum_out, update)
```

```python
import functools
import math

import jax
import jax.numpy as jnp
from jax import lax
from jax.experimental import pallas as pl
from jax.experimental.pallas import tpu as pltpu
from jax.sharding import PartitionSpec as P

BLOCK = 64
KEEP = 8
LANES = 128
SPAN = 1024
VMEM_BYTES = 16 * 1024 * 1024


def spans(cols):
    return [(start, min(SPAN, cols - start)) for start in range(0, cols, SPAN)]


def basis_tile(freq_ref):
    row = lax.broadcasted_iota(jnp.int32, (KEEP, LANES), 0)
    point = lax.broadcasted_iota(jnp.int32, (KEEP, LANES), 1) & (BLOCK - 1)
    freq = jnp.zeros((KEEP, LANES), jnp.int32)
    for k in range(KEEP):
        freq = jnp.where(row == k, freq_ref[k], freq)
    turn = ((2 * point + 1) * freq) & (4 * BLOCK - 1)
    turn = jnp.minimum(turn, 4 * BLOCK - turn)
    x = (BLOCK - turn).astype(jnp.float32) * (math.pi / (2 * BLOCK))
    y = x * x
    series = jnp.full_like(x, 1.0 / math.factorial(13))
    for n in (11, 9, 7, 5, 3, 1):
        series = 1.0 / math.factorial(n) - series * y
    scale = jnp.where(freq == 0, math.sqrt(1.0 / BLOCK), math.sqrt(2.0 / BLOCK))
    return x * series * scale


def split(v):
    high = v.astype(jnp.bfloat16)
    return high, (v - high.astype(jnp.float32)).astype(jnp.bfloat16)


def row_matrix(freq_ref):
    tile = basis_tile(freq_ref)
    lane = lax.broadcasted_iota(jnp.int32, (KEEP, LANES), 1)
    return jnp.concatenate([jnp.where(lane < BLOCK, tile, 0.0), jnp.where(lane >= BLOCK, tile, 0.0)], axis=0)


def col_matrix(freq_ref):
    tile = basis_tile(freq_ref)
    lane = lax.broadcasted_iota(jnp.int32, (KEEP, LANES), 1)
    left = jnp.where(lane < BLOCK, tile, 0.0)
    right = jnp.where(lane >= BLOCK, tile, 0.0)
    pair = jnp.concatenate([left, right], axis=0)
    none = jnp.zeros_like(pair)
    rows = []
    for t in range(SPAN // LANES):
        rows.append(jnp.concatenate([pair if u == t else none for u in range(SPAN // LANES)], axis=1))
    return split(jnp.concatenate(rows, axis=0))


def dot(a, b, dims):
    return lax.dot_general(a, b, (dims, ((), ())), preferred_element_type=jnp.float32)


def forward_kernel(fr_ref, fc_ref, m_ref, g_ref, out_ref, both, sems):
    cols = m_ref.shape[1]
    copies = []
    for n, (start, width) in enumerate(spans(cols)):
        for k, src in enumerate((m_ref, g_ref)):
            copy = pltpu.make_async_copy(
                src.at[:, pl.ds(start, width)], both.at[pl.ds(LANES * k, LANES), pl.ds(start, width)], sems.at[n, k]
            )
            copy.start()
            copies.append(copy)
    rows = row_matrix(fr_ref)
    high, low = split(jnp.concatenate([0.9 * rows, rows], axis=1))
    lhs = jnp.concatenate([high, low], axis=0)
    wide_high, wide_low = col_matrix(fc_ref)
    for n, (start, width) in enumerate(spans(cols)):
        copies[2 * n].wait()
        copies[2 * n + 1].wait()
        y = dot(lhs, both[:, start : start + width], ((1,), (0,)))
        y_high, y_low = split(y[:16] + y[16:])
        c = dot(jnp.concatenate([y_high, y_low], axis=0), wide_high[:, :width], ((1,), (1,)))
        c = c[:16] + c[16:] + dot(y_high, wide_low[:, :width], ((1,), (1,)))
        out_ref[:, n * LANES : (n + 1) * LANES] = c


def image_of(coeffs, row_stack, wide_high, wide_low, width):
    high, low = split(coeffs)
    z = dot(jnp.concatenate([high, low], axis=0), wide_high[:, :width], ((1,), (0,)))
    z = z[:16] + z[16:] + dot(high, wide_low[:, :width], ((1,), (0,)))
    z_high, z_low = split(z)
    return dot(row_stack, jnp.concatenate([z_high, z_low, z_high], axis=0), ((0,), (0,)))


def stack_rows(freq_ref):
    high, low = split(row_matrix(freq_ref))
    return jnp.concatenate([high, high, low], axis=0)


def momentum_kernel(fr_ref, fc_ref, m_ref, g_ref, c_ref, out_ref):
    row_stack = stack_rows(fr_ref)
    wide_high, wide_low = col_matrix(fc_ref)
    for n, (start, width) in enumerate(spans(m_ref.shape[1])):
        here = slice(start, start + width)
        image = image_of(c_ref[:, n * LANES : (n + 1) * LANES], row_stack, wide_high, wide_low, width)
        fresh = 0.9 * m_ref[:, here].astype(jnp.float32) + g_ref[:, here].astype(jnp.float32)
        out_ref[:, here] = (fresh - image).astype(jnp.bfloat16)


def update_kernel(entries, fr_ref, fc_ref, total_ref, p0, p1, p2, p3, out_ref, held, sems):
    row_stack = stack_rows(fr_ref)
    wide_high, wide_low = col_matrix(fc_ref)
    squares = jnp.sum(p0[...] + p1[...] + p2[...] + p3[...])
    scale = lax.rsqrt(jnp.full((16, LANES), squares, jnp.float32) * (1.0 / entries) + 1e-06)
    copies = []
    for n, (start, width) in enumerate(spans(out_ref.shape[1])):
        here = slice(start, start + width)
        part = total_ref[:, n * LANES : (n + 1) * LANES] * scale
        held[:, here] = image_of(part, row_stack, wide_high, wide_low, width)
        copy = pltpu.make_async_copy(held.at[:, pl.ds(start, width)], out_ref.at[:, pl.ds(start, width)], sems.at[n])
        copy.start()
        copies.append(copy)
    for copy in copies:
        copy.wait()


SMEM = pl.BlockSpec(memory_space=pltpu.SMEM)
VMEM = pl.BlockSpec(memory_space=pltpu.VMEM)
ANY = pl.BlockSpec(memory_space=pl.ANY)


def forward(freq_rows, freq_cols, m, g):
    rows, cols = m.shape
    n = len(spans(cols))
    return pl.pallas_call(
        forward_kernel,
        out_shape=jax.ShapeDtypeStruct((2 * KEEP, n * LANES), jnp.float32),
        in_specs=[SMEM, SMEM, ANY, ANY],
        out_specs=VMEM,
        scratch_shapes=[pltpu.VMEM((2 * rows, cols), jnp.bfloat16), pltpu.SemaphoreType.DMA((n, 2))],
        compiler_params=pltpu.CompilerParams(vmem_limit_bytes=VMEM_BYTES),
        cost_estimate=pl.CostEstimate(flops=2 * 48 * rows * cols, bytes_accessed=4 * rows * cols, transcendentals=0),
        name="forward",
    )(freq_rows, freq_cols, m, g)


def momentum_left(freq_rows, freq_cols, m, g, coeffs):
    rows, cols = m.shape
    return pl.pallas_call(
        momentum_kernel,
        out_shape=jax.ShapeDtypeStruct((rows, cols), jnp.bfloat16),
        in_specs=[SMEM, SMEM, VMEM, VMEM, VMEM],
        out_specs=VMEM,
        compiler_params=pltpu.CompilerParams(vmem_limit_bytes=VMEM_BYTES),
        cost_estimate=pl.CostEstimate(flops=2 * 48 * rows * cols, bytes_accessed=6 * rows * cols, transcendentals=0),
        name="momentum",
    )(freq_rows, freq_cols, m, g, coeffs)


def updated(freq_rows, freq_cols, total, parts, rows, cols, entries):
    n = len(spans(cols))
    return pl.pallas_call(
        functools.partial(update_kernel, entries),
        out_shape=jax.ShapeDtypeStruct((rows, cols), jnp.float32),
        in_specs=[SMEM, SMEM] + [VMEM] * 5,
        out_specs=ANY,
        scratch_shapes=[pltpu.VMEM((rows, cols), jnp.float32), pltpu.SemaphoreType.DMA((n,))],
        compiler_params=pltpu.CompilerParams(vmem_limit_bytes=VMEM_BYTES),
        cost_estimate=pl.CostEstimate(flops=2 * 48 * rows * cols, bytes_accessed=4 * rows * cols, transcendentals=0),
        name="update",
    )(freq_rows, freq_cols, total, *parts)


def exchange_sum(v, axes, members):
    return jnp.sum(lax.all_to_all(jnp.broadcast_to(v, (members,) + v.shape), axes, 0, 0, tiled=True), axis=0)


def body(momentum, grad, freq_rows, freq_cols):
    m, g = momentum[0], grad[0]
    rows, cols = m.shape
    tp = lax.axis_size("tp")
    own = forward(freq_rows, freq_cols, m, g)
    total = exchange_sum(exchange_sum(own, ("y", "x"), 8), ("z",), 8)
    tiles = (total * total).reshape(2, KEEP, total.shape[1])
    squares = tiles[0] + tiles[1]
    squares = sum(squares[:, k : k + LANES] for k in range(0, total.shape[1], LANES))
    parts = [squares] + [lax.ppermute(squares, "tp", [(i, i ^ k) for i in range(tp)]) for k in range(1, tp)]
    kept = momentum_left(freq_rows, freq_cols, m, g, own)
    update = updated(freq_rows, freq_cols, total, parts, rows, cols, float(rows * cols * tp))
    return kept[None], update


def solution(mesh):
    rep = ("z", "y", "x")
    fine = jax.sharding.Mesh(mesh.devices.reshape(8, 4, 2, 4), rep + ("tp",))
    placed = (P(rep, None, "tp"), P(rep, None, "tp"), P(), P())
    return jax.shard_map(
        body,
        mesh=fine,
        in_specs=placed,
        out_specs=(P(rep, None, "tp"), P(None, "tp")),
        check_vma=False,
    )
```

```python
import functools
import math

import jax
import jax.numpy as jnp
from jax import lax
from jax.experimental import pallas as pl
from jax.experimental.pallas import tpu as pltpu
from jax.sharding import PartitionSpec as P

BLOCK = 64
KEEP = 8
LANES = 128
SPAN = 1024
VMEM_BYTES = 16 * 1024 * 1024


def spans(cols):
    return [(start, min(SPAN, cols - start)) for start in range(0, cols, SPAN)]


def basis_tile(freq_ref):
    row = lax.broadcasted_iota(jnp.int32, (KEEP, LANES), 0)
    point = lax.broadcasted_iota(jnp.int32, (KEEP, LANES), 1) & (BLOCK - 1)
    freq = jnp.zeros((KEEP, LANES), jnp.int32)
    for k in range(KEEP):
        freq = jnp.where(row == k, freq_ref[k], freq)
    turn = ((2 * point + 1) * freq) & (4 * BLOCK - 1)
    turn = jnp.minimum(turn, 4 * BLOCK - turn)
    x = (BLOCK - turn).astype(jnp.float32) * (math.pi / (2 * BLOCK))
    y = x * x
    series = jnp.full_like(x, 1.0 / math.factorial(13))
    for n in (11, 9, 7, 5, 3, 1):
        series = 1.0 / math.factorial(n) - series * y
    scale = jnp.where(freq == 0, math.sqrt(1.0 / BLOCK), math.sqrt(2.0 / BLOCK))
    return x * series * scale


def split(v):
    high = v.astype(jnp.bfloat16)
    return high, (v - high.astype(jnp.float32)).astype(jnp.bfloat16)


def row_matrix(freq_ref):
    tile = basis_tile(freq_ref)
    lane = lax.broadcasted_iota(jnp.int32, (KEEP, LANES), 1)
    return jnp.concatenate([jnp.where(lane < BLOCK, tile, 0.0), jnp.where(lane >= BLOCK, tile, 0.0)], axis=0)


def col_matrix(freq_ref):
    tile = basis_tile(freq_ref)
    lane = lax.broadcasted_iota(jnp.int32, (KEEP, LANES), 1)
    left = jnp.where(lane < BLOCK, tile, 0.0)
    right = jnp.where(lane >= BLOCK, tile, 0.0)
    pair = jnp.concatenate([left, right], axis=0)
    none = jnp.zeros_like(pair)
    rows = []
    for t in range(SPAN // LANES):
        rows.append(jnp.concatenate([pair if u == t else none for u in range(SPAN // LANES)], axis=1))
    return split(jnp.concatenate(rows, axis=0))


def dot(a, b, dims):
    return lax.dot_general(a, b, (dims, ((), ())), preferred_element_type=jnp.float32)


def packed_rows(cols):
    whole, left = divmod(cols, SPAN)
    assert 0 < left <= SPAN // 2
    return 16 * whole + 8


def pack(spans16):
    last = spans16[-1]
    return jnp.concatenate(spans16[:-1] + [last[:8] + pltpu.roll(last[8:], LANES // 2, 1)], axis=0)


def unpack(rows):
    last = rows[-8:]
    return jnp.concatenate([rows, pltpu.roll(last, LANES // 2, 1)], axis=0)


def forward_kernel(
    fr_ref, fc_ref, m_ref, g_ref, out_ref, row_ref, high_ref, low_ref, both, fr_smem, fc_smem, fsems, sems
):
    cols = m_ref.shape[1]
    freqs = [
        pltpu.make_async_copy(src, dst, fsems.at[k]) for k, (src, dst) in enumerate(((fr_ref, fr_smem), (fc_ref, fc_smem)))
    ]
    for copy in freqs:
        copy.start()
    copies = []
    for n, (start, width) in enumerate(spans(cols)):
        for k, src in enumerate((m_ref, g_ref)):
            copy = pltpu.make_async_copy(
                src.at[:, pl.ds(start, width)], both.at[pl.ds(LANES * k, LANES), pl.ds(start, width)], sems.at[n, k]
            )
            copy.start()
            copies.append(copy)
    for copy in freqs:
        copy.wait()
    rows = row_matrix(fr_smem)
    high, low = split(jnp.concatenate([0.9 * rows, rows], axis=1))
    lhs = jnp.concatenate([high, low], axis=0)
    wide_high, wide_low = col_matrix(fc_smem)
    high_ref[...] = wide_high
    low_ref[...] = wide_low
    high, low = split(rows)
    stack = jnp.concatenate([high, high, low], axis=0).astype(jnp.float32)
    row_ref[...] = jnp.transpose(stack).astype(jnp.bfloat16)
    y_high, y_low = [], []
    for n, (start, width) in enumerate(spans(cols)):
        copies[2 * n].wait()
        copies[2 * n + 1].wait()
        y = dot(lhs, both[:, start : start + width], ((1,), (0,)))
        y = y[:16] + y[16:]
        if width < SPAN:
            y = jnp.concatenate([y, jnp.zeros((16, SPAN - width), jnp.float32)], axis=1)
        high, low = split(y)
        y_high.append(high)
        y_low.append(low)
    count = 16 * len(y_high)
    c = dot(jnp.concatenate(y_high + y_low, axis=0), wide_high, ((1,), (1,)))
    c = c[:count] + c[count:] + dot(jnp.concatenate(y_high, axis=0), wide_low, ((1,), (1,)))
    out_ref[...] = pack([c[k : k + 16] for k in range(0, count, 16)])


def half_image(rows, wide_high, wide_low):
    c = unpack(rows)
    count = c.shape[0]
    high, low = split(c)
    z = dot(jnp.concatenate([high, low], axis=0), wide_high, ((1,), (0,)))
    z = z[:count] + z[count:] + dot(high, wide_low, ((1,), (0,)))
    z_high, z_low = split(z)
    return [
        jnp.concatenate([z_high[k : k + 16], z_low[k : k + 16], z_high[k : k + 16]], axis=0) for k in range(0, count, 16)
    ]


def momentum_kernel(both, c_ref, row_ref, high_ref, low_ref, out_ref, held, sems):
    rows = row_ref[...]
    halves = half_image(c_ref[...], high_ref[...], low_ref[...])
    copies = []
    for n, (start, width) in enumerate(spans(out_ref.shape[1])):
        here = slice(start, start + width)
        image = dot(rows, halves[n][:, :width], ((1,), (0,)))
        fresh = 0.9 * both[:LANES, here].astype(jnp.float32) + both[LANES:, here].astype(jnp.float32)
        held[:, here] = (fresh - image).astype(jnp.bfloat16)
        copy = pltpu.make_async_copy(held.at[:, pl.ds(start, width)], out_ref.at[:, pl.ds(start, width)], sems.at[n])
        copy.start()
        copies.append(copy)
    for copy in copies:
        copy.wait()


def half_kernel(c_ref, high_ref, low_ref, out_ref):
    halves = half_image(c_ref[...], high_ref[...], low_ref[...])
    for n, (start, width) in enumerate(spans(out_ref.shape[1])):
        out_ref[:, start : start + width] = halves[n][:, :width]


def update_kernel(entries, row_ref, half_ref, p0, p1, p2, p3, out_ref, held, sems):
    rows = row_ref[...]
    squares = jnp.sum(p0[...] + p1[...] + p2[...] + p3[...])
    scale = lax.rsqrt(jnp.full((LANES, LANES), squares, jnp.float32) * (1.0 / entries) + 1e-06)
    copies = []
    for n, (start, width) in enumerate(spans(out_ref.shape[1])):
        here = slice(start, start + width)
        image = dot(rows, half_ref[:, here], ((1,), (0,)))
        held[:, here] = image * jnp.concatenate([scale] * (width // LANES), axis=1)
        copy = pltpu.make_async_copy(held.at[:, pl.ds(start, width)], out_ref.at[:, pl.ds(start, width)], sems.at[n])
        copy.start()
        copies.append(copy)
    for copy in copies:
        copy.wait()


VMEM = pl.BlockSpec(memory_space=pltpu.VMEM)
ANY = pl.BlockSpec(memory_space=pl.ANY)
PARAMS = pltpu.CompilerParams(vmem_limit_bytes=VMEM_BYTES)


def hbm(x):
    return pltpu.with_memory_space_constraint(x, pltpu.HBM)


def forward(freq_rows, freq_cols, m, g):
    rows, cols = m.shape
    n = len(spans(cols))
    return pl.pallas_call(
        forward_kernel,
        out_shape=[
            jax.ShapeDtypeStruct((packed_rows(cols), LANES), jnp.float32),
            pltpu.VMEM((rows, 48), jnp.bfloat16),
            pltpu.VMEM((LANES, SPAN), jnp.bfloat16),
            pltpu.VMEM((LANES, SPAN), jnp.bfloat16),
            pltpu.VMEM((2 * rows, cols), jnp.bfloat16),
        ],
        in_specs=[ANY] * 4,
        out_specs=[VMEM] * 5,
        scratch_shapes=[
            pltpu.SMEM((KEEP,), jnp.int32),
            pltpu.SMEM((KEEP,), jnp.int32),
            pltpu.SemaphoreType.DMA((2,)),
            pltpu.SemaphoreType.DMA((n, 2)),
        ],
        compiler_params=PARAMS,
        cost_estimate=pl.CostEstimate(flops=2 * 48 * rows * cols, bytes_accessed=4 * rows * cols, transcendentals=0),
        name="forward",
    )(hbm(freq_rows), hbm(freq_cols), hbm(m), hbm(g))


def momentum_left(both, coeffs, row, high, low):
    rows, cols = both.shape[0] // 2, both.shape[1]
    n = len(spans(cols))
    return pl.pallas_call(
        momentum_kernel,
        out_shape=jax.ShapeDtypeStruct((rows, cols), jnp.bfloat16),
        in_specs=[VMEM] * 5,
        out_specs=ANY,
        scratch_shapes=[pltpu.VMEM((rows, cols), jnp.bfloat16), pltpu.SemaphoreType.DMA((n,))],
        compiler_params=PARAMS,
        cost_estimate=pl.CostEstimate(flops=2 * 48 * rows * cols, bytes_accessed=2 * rows * cols, transcendentals=0),
        name="momentum",
    )(both, coeffs, row, high, low)


def half(total, high, low, cols):
    return pl.pallas_call(
        half_kernel,
        out_shape=pltpu.VMEM((48, cols), jnp.bfloat16),
        in_specs=[VMEM] * 3,
        out_specs=VMEM,
        compiler_params=PARAMS,
        cost_estimate=pl.CostEstimate(flops=2 * 48 * LANES * cols, bytes_accessed=1024, transcendentals=0),
        name="half",
    )(total, high, low)


def updated(row, halves, parts, entries):
    rows, cols = row.shape[0], halves.shape[1]
    n = len(spans(cols))
    return pl.pallas_call(
        functools.partial(update_kernel, entries),
        out_shape=jax.ShapeDtypeStruct((rows, cols), jnp.float32),
        in_specs=[VMEM] * 6,
        out_specs=ANY,
        scratch_shapes=[pltpu.VMEM((rows, cols), jnp.float32), pltpu.SemaphoreType.DMA((n,))],
        compiler_params=PARAMS,
        cost_estimate=pl.CostEstimate(flops=2 * 48 * rows * cols, bytes_accessed=4 * rows * cols, transcendentals=0),
        name="update",
    )(row, halves, *parts)


def moved(v, axis, pairs):
    return lax.ppermute(v, axis, pairs)


def replica_pairs(z, y, x):
    flip = (z * 4 + y) * 2 + x
    return [(r, r ^ flip) for r in range(64)]


def y_ring(step):
    return [(r, r // 8 * 8 + (r % 8 + 2 * step) % 8) for r in range(64)]


def four_way(v, a, b):
    both = tuple(i ^ j for i, j in zip(a, b))
    return (v + moved(v, "rep", replica_pairs(*a))) + (
        moved(v, "rep", replica_pairs(*b)) + moved(v, "rep", replica_pairs(*both))
    )


def body(momentum, grad, freq_rows, freq_cols):
    m, g = momentum[0], grad[0]
    rows, cols = m.shape
    tp = lax.axis_size("tp")
    own, row, high, low, both = forward(freq_rows, freq_cols, m, g)
    total = own + moved(own, "rep", y_ring(1)) + moved(own, "rep", y_ring(3)) + moved(own, "rep", y_ring(2))
    total = four_way(total, (1, 0, 0), (2, 0, 0))
    total = total + moved(total, "rep", replica_pairs(6, 0, 0))
    total = total + moved(total, "rep", replica_pairs(0, 0, 1))
    squares = total * total
    squares = sum(squares[k : k + KEEP] for k in range(0, total.shape[0], KEEP))
    parts = [squares] + [moved(squares, "tp", [(i, i ^ k) for i in range(tp)]) for k in range(1, tp)]
    kept = momentum_left(both, own, row, high, low)
    update = updated(row, half(total, high, low, cols), parts, float(rows * cols * tp))
    return kept[None], update


def solution(mesh):
    placed = (P("rep", None, "tp"), P("rep", None, "tp"), P(), P())
    return jax.shard_map(
        body,
        mesh=mesh,
        in_specs=placed,
        out_specs=(P("rep", None, "tp"), P(None, "tp")),
        check_vma=False,
    )
```

```python
import functools
import math

import jax
import jax.numpy as jnp
from jax import lax
from jax.experimental import pallas as pl
from jax.experimental.pallas import tpu as pltpu
from jax.sharding import PartitionSpec as P

BLOCK = 64
KEEP = 8
LANES = 128
SPAN = 1024
VMEM_BYTES = 16 * 1024 * 1024


def spans(cols):
    return [(start, min(SPAN, cols - start)) for start in range(0, cols, SPAN)]


def basis_tile(freq_ref):
    row = lax.broadcasted_iota(jnp.int32, (KEEP, LANES), 0)
    point = lax.broadcasted_iota(jnp.int32, (KEEP, LANES), 1) & (BLOCK - 1)
    freq = jnp.zeros((KEEP, LANES), jnp.int32)
    for k in range(KEEP):
        freq = jnp.where(row == k, freq_ref[k], freq)
    turn = ((2 * point + 1) * freq) & (4 * BLOCK - 1)
    turn = jnp.minimum(turn, 4 * BLOCK - turn)
    x = (BLOCK - turn).astype(jnp.float32) * (math.pi / (2 * BLOCK))
    y = x * x
    series = jnp.full_like(x, 1.0 / math.factorial(13))
    for n in (11, 9, 7, 5, 3, 1):
        series = 1.0 / math.factorial(n) - series * y
    scale = jnp.where(freq == 0, math.sqrt(1.0 / BLOCK), math.sqrt(2.0 / BLOCK))
    return x * series * scale


def split(v):
    high = v.astype(jnp.bfloat16)
    return high, (v - high.astype(jnp.float32)).astype(jnp.bfloat16)


def row_matrix(freq_ref):
    tile = basis_tile(freq_ref)
    lane = lax.broadcasted_iota(jnp.int32, (KEEP, LANES), 1)
    return jnp.concatenate([jnp.where(lane < BLOCK, tile, 0.0), jnp.where(lane >= BLOCK, tile, 0.0)], axis=0)


def col_matrix(freq_ref):
    tile = basis_tile(freq_ref)
    lane = lax.broadcasted_iota(jnp.int32, (KEEP, LANES), 1)
    left = jnp.where(lane < BLOCK, tile, 0.0)
    right = jnp.where(lane >= BLOCK, tile, 0.0)
    pair = jnp.concatenate([left, right], axis=0)
    none = jnp.zeros_like(pair)
    rows = []
    for t in range(SPAN // LANES):
        rows.append(jnp.concatenate([pair if u == t else none for u in range(SPAN // LANES)], axis=1))
    return split(jnp.concatenate(rows, axis=0))


def dot(a, b, dims):
    return lax.dot_general(a, b, (dims, ((), ())), preferred_element_type=jnp.float32)


def packed_rows(cols):
    whole, left = divmod(cols, SPAN)
    assert 0 < left <= SPAN // 2
    return 16 * whole + 8


def pack(spans16):
    last = spans16[-1]
    return jnp.concatenate(spans16[:-1] + [last[:8] + pltpu.roll(last[8:], LANES // 2, 1)], axis=0)


def unpack(rows):
    last = rows[-8:]
    return jnp.concatenate([rows, pltpu.roll(last, LANES // 2, 1)], axis=0)


def forward_kernel(
    fr_ref, fc_ref, m_ref, g_ref, out_ref, row_ref, high_ref, low_ref, both, fr_smem, fc_smem, fsems, sems
):
    cols = m_ref.shape[1]
    freqs = [
        pltpu.make_async_copy(src, dst, fsems.at[k]) for k, (src, dst) in enumerate(((fr_ref, fr_smem), (fc_ref, fc_smem)))
    ]
    for copy in freqs:
        copy.start()
    copies = []
    for n, (start, width) in enumerate(spans(cols)):
        for k, src in enumerate((m_ref, g_ref)):
            copy = pltpu.make_async_copy(
                src.at[:, pl.ds(start, width)], both.at[pl.ds(LANES * k, LANES), pl.ds(start, width)], sems.at[n, k]
            )
            copy.start()
            copies.append(copy)
    for copy in freqs:
        copy.wait()
    rows = row_matrix(fr_smem)
    high, low = split(jnp.concatenate([0.9 * rows, rows], axis=1))
    lhs = jnp.concatenate([high, low], axis=0)
    wide_high, wide_low = col_matrix(fc_smem)
    high_ref[...] = wide_high
    low_ref[...] = wide_low
    high, low = split(rows)
    stack = jnp.concatenate([high, high, low], axis=0).astype(jnp.float32)
    row_ref[...] = jnp.transpose(stack).astype(jnp.bfloat16)
    y_high, y_low = [], []
    for n, (start, width) in enumerate(spans(cols)):
        copies[2 * n].wait()
        copies[2 * n + 1].wait()
        y = dot(lhs, both[:, start : start + width], ((1,), (0,)))
        y = y[:16] + y[16:]
        if width < SPAN:
            y = jnp.concatenate([y, jnp.zeros((16, SPAN - width), jnp.float32)], axis=1)
        high, low = split(y)
        y_high.append(high)
        y_low.append(low)
    count = 16 * len(y_high)
    c = dot(jnp.concatenate(y_high + y_low, axis=0), wide_high, ((1,), (1,)))
    c = c[:count] + c[count:] + dot(jnp.concatenate(y_high, axis=0), wide_low, ((1,), (1,)))
    out_ref[...] = pack([c[k : k + 16] for k in range(0, count, 16)])


def half_image(rows, wide_high, wide_low):
    c = unpack(rows)
    count = c.shape[0]
    high, low = split(c)
    z = dot(jnp.concatenate([high, low], axis=0), wide_high, ((1,), (0,)))
    z = z[:count] + z[count:] + dot(high, wide_low, ((1,), (0,)))
    z_high, z_low = split(z)
    return [
        jnp.concatenate([z_high[k : k + 16], z_low[k : k + 16], z_high[k : k + 16]], axis=0) for k in range(0, count, 16)
    ]


def momentum_kernel(both, c_ref, row_ref, high_ref, low_ref, out_ref, held, sems):
    rows = row_ref[...]
    halves = half_image(c_ref[...], high_ref[...], low_ref[...])
    copies = []
    for n, (start, width) in enumerate(spans(out_ref.shape[1])):
        here = slice(start, start + width)
        image = dot(rows, halves[n][:, :width], ((1,), (0,)))
        fresh = 0.9 * both[:LANES, here].astype(jnp.float32) + both[LANES:, here].astype(jnp.float32)
        held[:, here] = (fresh - image).astype(jnp.bfloat16)
        copy = pltpu.make_async_copy(held.at[:, pl.ds(start, width)], out_ref.at[:, pl.ds(start, width)], sems.at[n])
        copy.start()
        copies.append(copy)
    for copy in copies:
        copy.wait()


def half_kernel(c_ref, high_ref, low_ref, out_ref):
    halves = half_image(c_ref[...], high_ref[...], low_ref[...])
    for n, (start, width) in enumerate(spans(out_ref.shape[1])):
        out_ref[:, start : start + width] = halves[n][:, :width]


def update_kernel(entries, row_ref, half_ref, squares_ref, out_ref, held, sems):
    rows = row_ref[...]
    squares = jnp.sum(squares_ref[...])
    scale = lax.rsqrt(jnp.full((LANES, LANES), squares, jnp.float32) * (1.0 / entries) + 1e-06)
    copies = []
    for n, (start, width) in enumerate(spans(out_ref.shape[1])):
        here = slice(start, start + width)
        image = dot(rows, half_ref[:, here], ((1,), (0,)))
        held[:, here] = image * jnp.concatenate([scale] * (width // LANES), axis=1)
        copy = pltpu.make_async_copy(held.at[:, pl.ds(start, width)], out_ref.at[:, pl.ds(start, width)], sems.at[n])
        copy.start()
        copies.append(copy)
    for copy in copies:
        copy.wait()


VMEM = pl.BlockSpec(memory_space=pltpu.VMEM)
ANY = pl.BlockSpec(memory_space=pl.ANY)
PARAMS = pltpu.CompilerParams(vmem_limit_bytes=VMEM_BYTES)


def hbm(x):
    return pltpu.with_memory_space_constraint(x, pltpu.HBM)


def forward(freq_rows, freq_cols, m, g):
    rows, cols = m.shape
    n = len(spans(cols))
    return pl.pallas_call(
        forward_kernel,
        out_shape=[
            jax.ShapeDtypeStruct((packed_rows(cols), LANES), jnp.float32),
            pltpu.VMEM((rows, 48), jnp.bfloat16),
            pltpu.VMEM((LANES, SPAN), jnp.bfloat16),
            pltpu.VMEM((LANES, SPAN), jnp.bfloat16),
            pltpu.VMEM((2 * rows, cols), jnp.bfloat16),
        ],
        in_specs=[ANY] * 4,
        out_specs=[VMEM] * 5,
        scratch_shapes=[
            pltpu.SMEM((KEEP,), jnp.int32),
            pltpu.SMEM((KEEP,), jnp.int32),
            pltpu.SemaphoreType.DMA((2,)),
            pltpu.SemaphoreType.DMA((n, 2)),
        ],
        compiler_params=PARAMS,
        cost_estimate=pl.CostEstimate(flops=2 * 48 * rows * cols, bytes_accessed=4 * rows * cols, transcendentals=0),
        name="forward",
    )(hbm(freq_rows), hbm(freq_cols), hbm(m), hbm(g))


def momentum_left(both, coeffs, row, high, low):
    rows, cols = both.shape[0] // 2, both.shape[1]
    n = len(spans(cols))
    return pl.pallas_call(
        momentum_kernel,
        out_shape=jax.ShapeDtypeStruct((rows, cols), jnp.bfloat16),
        in_specs=[VMEM] * 5,
        out_specs=ANY,
        scratch_shapes=[pltpu.VMEM((rows, cols), jnp.bfloat16), pltpu.SemaphoreType.DMA((n,))],
        compiler_params=PARAMS,
        cost_estimate=pl.CostEstimate(flops=2 * 48 * rows * cols, bytes_accessed=2 * rows * cols, transcendentals=0),
        name="momentum",
    )(both, coeffs, row, high, low)


def half(total, high, low, cols):
    return pl.pallas_call(
        half_kernel,
        out_shape=pltpu.VMEM((48, cols), jnp.bfloat16),
        in_specs=[VMEM] * 3,
        out_specs=VMEM,
        compiler_params=PARAMS,
        cost_estimate=pl.CostEstimate(flops=2 * 48 * LANES * cols, bytes_accessed=1024, transcendentals=0),
        name="half",
    )(total, high, low)


def updated(row, halves, squares, entries):
    rows, cols = row.shape[0], halves.shape[1]
    n = len(spans(cols))
    return pl.pallas_call(
        functools.partial(update_kernel, entries),
        out_shape=jax.ShapeDtypeStruct((rows, cols), jnp.float32),
        in_specs=[VMEM] * 3,
        out_specs=ANY,
        scratch_shapes=[pltpu.VMEM((rows, cols), jnp.float32), pltpu.SemaphoreType.DMA((n,))],
        compiler_params=PARAMS,
        cost_estimate=pl.CostEstimate(flops=2 * 48 * rows * cols, bytes_accessed=4 * rows * cols, transcendentals=0),
        name="update",
    )(row, halves, squares)


def moved(v, partner):
    pairs = []
    for d in range(256):
        z, y, x, near, core = d // 32, d // 8 % 4, d // 4 % 2, d // 2 % 2, d % 2
        z, y, x, near, core = partner(z, y, x, near, core)
        pairs.append((d, (((z * 4 + y) * 2 + x) * 2 + near) * 2 + core))
    return lax.ppermute(v, ("rep", "tp"), pairs)


def replica(dz, dy, dx):
    def partner(z, y, x, near, core):
        if core == 0:
            return (z ^ 1, y, x, near, core) if dy else (z, y ^ 1, x, near, core)
        return z ^ dz, y ^ dy, x ^ dx, near, core

    return partner


def other_core(z, y, x, near, core):
    return z, y, x, near, 1 - core


def next_chip(z, y, x, near, core):
    return z, y, x, 1 - near, core


def four_way(v, a, b):
    both = tuple(i ^ j for i, j in zip(a, b))
    return (v + moved(v, replica(*a))) + (moved(v, replica(*b)) + moved(v, replica(*both)))


def body(momentum, grad, freq_rows, freq_cols):
    m, g = momentum[0], grad[0]
    rows, cols = m.shape
    tp = lax.axis_size("tp")
    core = lax.axis_index("tp") % 2
    own, row, high, low, both = forward(freq_rows, freq_cols, m, g)
    count = own.shape[0]
    other = moved(own, other_core)
    pair = jnp.concatenate([jnp.where(core == 1, other, own), jnp.where(core == 1, own, other)], axis=0)
    pair = four_way(pair, (0, 1, 0), (0, 2, 0))
    pair = four_way(pair, (1, 0, 0), (3, 0, 0))
    pair = pair + moved(pair, replica(6, 0, 0))
    kept = momentum_left(both, own, row, high, low)
    other, kept = lax.optimization_barrier((moved(pair, replica(0, 0, 1)), kept))
    pair = pair + other
    squares = pair * pair
    squares = sum(squares[k : k + KEEP] for k in range(0, 2 * count, KEEP))
    squares = squares + moved(squares, next_chip)
    sent = jnp.concatenate([pair[:count], squares], axis=0)
    sent = jnp.where(core == 1, jnp.concatenate([pair[count:], squares], axis=0), moved(sent, other_core))
    halves = half(sent[:count], high, low, cols)
    squares = sent[count:]
    update = updated(row, halves, squares, float(rows * cols * tp))
    return kept[None], update


def solution(mesh):
    placed = (P("rep", None, "tp"), P("rep", None, "tp"), P(), P())
    return jax.shard_map(
        body,
        mesh=mesh,
        in_specs=placed,
        out_specs=(P("rep", None, "tp"), P(None, "tp")),
        check_vma=False,
    )
```

```python
import functools
import math

import jax
import jax.numpy as jnp
from jax import lax
from jax.experimental import pallas as pl
from jax.experimental.pallas import tpu as pltpu
from jax.sharding import PartitionSpec as P

BLOCK = 64
KEEP = 8
LANES = 128
SPAN = 1024
VMEM_BYTES = 16 * 1024 * 1024
TILES = SPAN // LANES
WRITES = [(0, 512), (512, 1024), (1536, 1920)]
READS = [(0, 2048), (2048, 1408)]


def spans(cols):
    return [(start, min(SPAN, cols - start)) for start in range(0, cols, SPAN)]


def basis_tiles(fr_ref, fc_ref):
    row = lax.broadcasted_iota(jnp.int32, (2 * KEEP, LANES), 0)
    point = lax.broadcasted_iota(jnp.int32, (2 * KEEP, LANES), 1) & (BLOCK - 1)
    freq = jnp.zeros((2 * KEEP, LANES), jnp.int32)
    for k in range(KEEP):
        freq = jnp.where(row == k, fr_ref[k], freq)
        freq = jnp.where(row == KEEP + k, fc_ref[k], freq)
    turn = ((2 * point + 1) * freq) & (4 * BLOCK - 1)
    turn = jnp.minimum(turn, 4 * BLOCK - turn)
    x = (BLOCK - turn).astype(jnp.float32) * (math.pi / (2 * BLOCK))
    y = x * x
    series = jnp.full_like(x, 1.0 / math.factorial(13))
    for n in (11, 9, 7, 5, 3, 1):
        series = 1.0 / math.factorial(n) - series * y
    scale = jnp.where(freq == 0, math.sqrt(1.0 / BLOCK), math.sqrt(2.0 / BLOCK))
    return x * series * scale


def split(v):
    high = v.astype(jnp.bfloat16)
    return high, (v - high.astype(jnp.float32)).astype(jnp.bfloat16)


def two_blocks(tile):
    lane = lax.broadcasted_iota(jnp.int32, (KEEP, LANES), 1)
    return jnp.concatenate([jnp.where(lane < BLOCK, tile, 0.0), jnp.where(lane >= BLOCK, tile, 0.0)], axis=0)


def only(t, v):
    lane = lax.broadcasted_iota(jnp.int32, v.shape, 1)
    return jnp.where((lane >> 4) == t, v, 0.0)


def dot(a, b, dims):
    return lax.dot_general(a, b, (dims, ((), ())), preferred_element_type=jnp.float32)


def packed_rows(cols):
    whole, left = divmod(cols, SPAN)
    assert 0 < left <= SPAN // 2
    return 16 * whole + 8


def pack(spans16):
    last = spans16[-1]
    return jnp.concatenate(spans16[:-1] + [last[:8] + pltpu.roll(last[8:], LANES // 2, 1)], axis=0)


def unpack(rows):
    last = rows[-8:]
    return jnp.concatenate([rows, pltpu.roll(last, LANES // 2, 1)], axis=0)


def forward_kernel(
    fr_ref, fc_ref, m_ref, g_ref, out_ref, row_ref, high_ref, low_ref, both, fr_smem, fc_smem, fsems, sems
):
    cols = m_ref.shape[1]
    freqs = [
        pltpu.make_async_copy(src, dst, fsems.at[k]) for k, (src, dst) in enumerate(((fr_ref, fr_smem), (fc_ref, fc_smem)))
    ]
    for copy in freqs:
        copy.start()
    copies = []
    for n, (start, width) in enumerate(READS):
        for k, src in enumerate((m_ref, g_ref)):
            copy = pltpu.make_async_copy(
                src.at[:, pl.ds(start, width)], both.at[pl.ds(LANES * k, LANES), pl.ds(start, width)], sems.at[n, k]
            )
            copy.start()
            copies.append(copy)
    for copy in freqs:
        copy.wait()
    tiles = basis_tiles(fr_smem, fc_smem)
    rows = two_blocks(tiles[:KEEP])
    row_ref[...] = rows
    high, low = split(jnp.concatenate([0.9 * rows, rows], axis=1))
    lhs = jnp.concatenate([high, low], axis=0)
    high, low = split(two_blocks(tiles[KEEP:]))
    high_ref[...] = jnp.concatenate([high] * TILES, axis=0)
    low_ref[...] = jnp.concatenate([low] * TILES, axis=0)
    high_tiles, low_tiles = [], []
    for n, (start, width) in enumerate(READS):
        copies[2 * n].wait()
        copies[2 * n + 1].wait()
        y = dot(lhs, both[:, start : start + width], ((1,), (0,)))
        high, low = split(y[:16] + y[16:])
        high_tiles += [high[:, k : k + LANES] for k in range(0, width, LANES)]
        low_tiles += [low[:, k : k + LANES] for k in range(0, width, LANES)]
    y_high = jnp.concatenate(high_tiles, axis=0)
    c = dot(jnp.concatenate([y_high] + low_tiles, axis=0), high_ref[...], ((1,), (1,)))
    c = c[: y_high.shape[0]] + c[y_high.shape[0] :] + dot(y_high, low_ref[...], ((1,), (1,)))
    sums = []
    for first in range(0, cols // LANES, TILES):
        parts = [only(t - first, c[16 * t : 16 * t + 16]) for t in range(first, min(first + TILES, cols // LANES))]
        while len(parts) > 1:
            parts = [sum(parts[k : k + 2]) for k in range(0, len(parts), 2)]
        sums.append(parts[0])
    out_ref[...] = pack(sums)


def half_image(c, high_ref, low_ref, tiles):
    high = c.astype(jnp.bfloat16).astype(jnp.float32)
    low = c - high

    def spread(v):
        return jnp.concatenate(
            [only(t % TILES, v[t // TILES * 16 : t // TILES * 16 + 16]).astype(jnp.bfloat16) for t in tiles], axis=0
        )

    high = spread(high)
    count = high.shape[0]
    z = dot(jnp.concatenate([high, spread(low)], axis=0), high_ref[...], ((1,), (0,)))
    z = z[:count] + z[count:] + dot(high, low_ref[...], ((1,), (0,)))
    z_high, z_low = split(z)
    return jnp.concatenate(
        [jnp.concatenate([z_high[k : k + 16], z_low[k : k + 16], z_high[k : k + 16]], axis=0) for k in range(0, count, 16)],
        axis=1,
    )


def momentum_kernel(both, c_ref, row_ref, high_ref, low_ref, out_ref, turned_ref, held, sems):
    high, low = split(jnp.transpose(jnp.concatenate([row_ref[...]] * 3, axis=0)))
    third = lax.broadcasted_iota(jnp.int32, high.shape, 1) >= 32
    rows = jnp.where(third, low.astype(jnp.float32), high.astype(jnp.float32)).astype(jnp.bfloat16)
    turned_ref[...] = rows
    halves = half_image(unpack(c_ref[...]), high_ref, low_ref, range(out_ref.shape[1] // LANES))
    copies = []
    for n, (start, width) in enumerate(spans(out_ref.shape[1])):
        here = slice(start, start + width)
        image = dot(rows, halves[:, here], ((1,), (0,)))
        fresh = 0.9 * both[:LANES, here].astype(jnp.float32) + both[LANES:, here].astype(jnp.float32)
        held[:, here] = (fresh - image).astype(jnp.bfloat16)
        copy = pltpu.make_async_copy(held.at[:, pl.ds(start, width)], out_ref.at[:, pl.ds(start, width)], sems.at[n])
        copy.start()
        copies.append(copy)
    for copy in copies:
        copy.wait()


def update_kernel(entries, sent_ref, row_ref, high_ref, low_ref, out_ref, held, sems):
    rows = row_ref[...]
    count = sent_ref.shape[0] - KEEP
    c = unpack(sent_ref[:count])
    squares = jnp.sum(sent_ref[count:])
    scale = lax.rsqrt(jnp.full((LANES, LANES), squares, jnp.float32) * (1.0 / entries) + 1e-06)
    first = WRITES[0][1]
    halves = [
        half_image(c, high_ref, low_ref, range(first // LANES)),
        half_image(c, high_ref, low_ref, range(first // LANES, out_ref.shape[1] // LANES)),
    ]
    copies = []
    for n, (start, width) in enumerate(WRITES):
        here = slice(start, start + width)
        half = halves[0] if n == 0 else halves[1][:, start - first : start - first + width]
        image = dot(rows, half, ((1,), (0,)))
        held[:, here] = image * jnp.concatenate([scale] * (width // LANES), axis=1)
        copy = pltpu.make_async_copy(held.at[:, pl.ds(start, width)], out_ref.at[:, pl.ds(start, width)], sems.at[n])
        copy.start()
        copies.append(copy)
    for copy in copies:
        copy.wait()


VMEM = pl.BlockSpec(memory_space=pltpu.VMEM)
ANY = pl.BlockSpec(memory_space=pl.ANY)
PARAMS = pltpu.CompilerParams(vmem_limit_bytes=VMEM_BYTES)


def hbm(x):
    return pltpu.with_memory_space_constraint(x, pltpu.HBM)


def forward(freq_rows, freq_cols, m, g):
    rows, cols = m.shape
    return pl.pallas_call(
        forward_kernel,
        out_shape=[
            jax.ShapeDtypeStruct((packed_rows(cols), LANES), jnp.float32),
            pltpu.VMEM((16, LANES), jnp.float32),
            pltpu.VMEM((LANES, LANES), jnp.bfloat16),
            pltpu.VMEM((LANES, LANES), jnp.bfloat16),
            pltpu.VMEM((2 * rows, cols), jnp.bfloat16),
        ],
        in_specs=[ANY] * 4,
        out_specs=[VMEM] * 5,
        scratch_shapes=[
            pltpu.SMEM((KEEP,), jnp.int32),
            pltpu.SMEM((KEEP,), jnp.int32),
            pltpu.SemaphoreType.DMA((2,)),
            pltpu.SemaphoreType.DMA((len(READS), 2)),
        ],
        compiler_params=PARAMS,
        cost_estimate=pl.CostEstimate(flops=2 * 48 * rows * cols, bytes_accessed=4 * rows * cols, transcendentals=0),
        name="forward",
    )(hbm(freq_rows), hbm(freq_cols), hbm(m), hbm(g))


def momentum_left(both, coeffs, row, high, low):
    rows, cols = both.shape[0] // 2, both.shape[1]
    n = len(spans(cols))
    return pl.pallas_call(
        momentum_kernel,
        out_shape=[jax.ShapeDtypeStruct((rows, cols), jnp.bfloat16), pltpu.VMEM((rows, 48), jnp.bfloat16)],
        in_specs=[VMEM] * 5,
        out_specs=[ANY, VMEM],
        scratch_shapes=[pltpu.VMEM((rows, cols), jnp.bfloat16), pltpu.SemaphoreType.DMA((len(spans(cols)),))],
        compiler_params=PARAMS,
        cost_estimate=pl.CostEstimate(flops=2 * 48 * rows * cols, bytes_accessed=2 * rows * cols, transcendentals=0),
        name="momentum",
    )(both, coeffs, row, high, low)


def updated(sent, row, high, low, cols, entries):
    rows = row.shape[0]
    return pl.pallas_call(
        functools.partial(update_kernel, entries),
        out_shape=jax.ShapeDtypeStruct((rows, cols), jnp.float32),
        in_specs=[VMEM] * 4,
        out_specs=ANY,
        scratch_shapes=[pltpu.VMEM((rows, cols), jnp.float32), pltpu.SemaphoreType.DMA((len(WRITES),))],
        compiler_params=PARAMS,
        cost_estimate=pl.CostEstimate(flops=2 * 48 * rows * cols, bytes_accessed=4 * rows * cols, transcendentals=0),
        name="update",
    )(sent, row, high, low)


def moved(v, partner):
    pairs = []
    for d in range(256):
        z, y, x, near, core = d // 32, d // 8 % 4, d // 4 % 2, d // 2 % 2, d % 2
        z, y, x, near, core = partner(z, y, x, near, core)
        pairs.append((d, (((z * 4 + y) * 2 + x) * 2 + near) * 2 + core))
    return lax.ppermute(v, ("rep", "tp"), pairs)


def replica(dz, dy, dx):
    def partner(z, y, x, near, core):
        if core == 0:
            return (z ^ 1, y, x, near, core) if dy else (z, y ^ 1, x, near, core)
        return z ^ dz, y ^ dy, x ^ dx, near, core

    return partner


def other_core(z, y, x, near, core):
    return z, y, x, near, 1 - core


def next_chip(z, y, x, near, core):
    return z, y, x, 1 - near, core


def four_way(v, a, b):
    both = tuple(i ^ j for i, j in zip(a, b))
    return (v + moved(v, replica(*a))) + (moved(v, replica(*b)) + moved(v, replica(*both)))


def body(momentum, grad, freq_rows, freq_cols):
    m, g = momentum[0], grad[0]
    rows, cols = m.shape
    tp = lax.axis_size("tp")
    core = lax.axis_index("tp") % 2
    own, row, high, low, both = forward(freq_rows, freq_cols, m, g)
    count = own.shape[0]
    other = moved(own, other_core)
    pair = jnp.concatenate([jnp.where(core == 1, other, own), jnp.where(core == 1, own, other)], axis=0)
    pair = four_way(pair, (0, 1, 0), (0, 2, 0))
    pair = four_way(pair, (1, 0, 0), (3, 0, 0))
    pair = pair + moved(pair, replica(6, 0, 0))
    kept, turned = momentum_left(both, own, row, high, low)
    other, kept, turned = lax.optimization_barrier((moved(pair, replica(0, 0, 1)), kept, turned))
    pair = pair + other
    squares = pair * pair
    squares = sum(squares[k : k + KEEP] for k in range(0, 2 * count, KEEP))
    squares = squares + moved(squares, next_chip)
    sent = jnp.concatenate([pair[:count], squares], axis=0)
    sent = jnp.where(core == 1, jnp.concatenate([pair[count:], squares], axis=0), moved(sent, other_core))
    update = updated(sent, turned, high, low, cols, float(rows * cols * tp))
    return kept[None], update


def solution(mesh):
    placed = (P("rep", None, "tp"), P("rep", None, "tp"), P(), P())
    return jax.shard_map(
        body,
        mesh=mesh,
        in_specs=placed,
        out_specs=(P("rep", None, "tp"), P(None, "tp")),
        check_vma=False,
    )
```

```python
import functools
import math

import jax
import jax.numpy as jnp
from jax import lax
from jax.experimental import pallas as pl
from jax.experimental.pallas import tpu as pltpu
from jax.sharding import PartitionSpec as P

BLOCK = 64
KEEP = 8
LANES = 128
SPAN = 1024
VMEM_BYTES = 16 * 1024 * 1024
TILES = SPAN // LANES
WRITES = [(0, 512), (512, 1024), (1536, 1920)]
READS = [(0, 2048), (2048, 1408)]


def spans(cols):
    return [(start, min(SPAN, cols - start)) for start in range(0, cols, SPAN)]


def basis_tiles(fr_ref, fc_ref):
    row = lax.broadcasted_iota(jnp.int32, (2 * KEEP, LANES), 0)
    point = lax.broadcasted_iota(jnp.int32, (2 * KEEP, LANES), 1) & (BLOCK - 1)
    freq = jnp.zeros((2 * KEEP, LANES), jnp.int32)
    for k in range(KEEP):
        freq = jnp.where(row == k, fr_ref[k], freq)
        freq = jnp.where(row == KEEP + k, fc_ref[k], freq)
    turn = ((2 * point + 1) * freq) & (4 * BLOCK - 1)
    turn = jnp.minimum(turn, 4 * BLOCK - turn)
    x = (BLOCK - turn).astype(jnp.float32) * (math.pi / (2 * BLOCK))
    y = x * x
    series = jnp.full_like(x, 1.0 / math.factorial(13))
    for n in (11, 9, 7, 5, 3, 1):
        series = 1.0 / math.factorial(n) - series * y
    scale = jnp.where(freq == 0, math.sqrt(1.0 / BLOCK), math.sqrt(2.0 / BLOCK))
    return x * series * scale


def split(v):
    high = v.astype(jnp.bfloat16)
    return high, (v - high.astype(jnp.float32)).astype(jnp.bfloat16)


def two_blocks(tile):
    lane = lax.broadcasted_iota(jnp.int32, (KEEP, LANES), 1)
    return jnp.concatenate([jnp.where(lane < BLOCK, tile, 0.0), jnp.where(lane >= BLOCK, tile, 0.0)], axis=0)


def only(t, v):
    lane = lax.broadcasted_iota(jnp.int32, v.shape, 1)
    return jnp.where((lane >> 4) == t, v, 0.0)


def dot(a, b, dims):
    return lax.dot_general(a, b, (dims, ((), ())), preferred_element_type=jnp.float32)


def packed_rows(cols):
    whole, left = divmod(cols, SPAN)
    assert 0 < left <= SPAN // 2
    return 16 * whole + 8


def pack(spans16):
    last = spans16[-1]
    return jnp.concatenate(spans16[:-1] + [last[:8] + pltpu.roll(last[8:], LANES // 2, 1)], axis=0)


def unpack(rows):
    last = rows[-8:]
    return jnp.concatenate([rows, pltpu.roll(last, LANES // 2, 1)], axis=0)


def forward_kernel(
    fr_ref, fc_ref, m_ref, g_ref, out_ref, row_ref, high_ref, low_ref, both, fr_smem, fc_smem, fsems, sems
):
    cols = m_ref.shape[1]
    freqs = [
        pltpu.make_async_copy(src, dst, fsems.at[k]) for k, (src, dst) in enumerate(((fr_ref, fr_smem), (fc_ref, fc_smem)))
    ]
    for copy in freqs:
        copy.start()
    copies = []
    for n, (start, width) in enumerate(READS):
        for k, src in enumerate((m_ref, g_ref)):
            copy = pltpu.make_async_copy(
                src.at[:, pl.ds(start, width)], both.at[pl.ds(LANES * k, LANES), pl.ds(start, width)], sems.at[n, k]
            )
            copy.start()
            copies.append(copy)
    for copy in freqs:
        copy.wait()
    tiles = basis_tiles(fr_smem, fc_smem)
    rows = two_blocks(tiles[:KEEP])
    row_ref[...] = rows
    high, low = split(jnp.concatenate([0.9 * rows, rows], axis=1))
    lhs = jnp.concatenate([high, low], axis=0)
    high, low = split(two_blocks(tiles[KEEP:]))
    high_ref[...] = jnp.concatenate([high] * TILES, axis=0)
    low_ref[...] = jnp.concatenate([low] * TILES, axis=0)
    high_tiles, low_tiles = [], []
    for n, (start, width) in enumerate(READS):
        copies[2 * n].wait()
        copies[2 * n + 1].wait()
        y = dot(lhs, both[:, start : start + width], ((1,), (0,)))
        high, low = split(y[:16] + y[16:])
        high_tiles += [high[:, k : k + LANES] for k in range(0, width, LANES)]
        low_tiles += [low[:, k : k + LANES] for k in range(0, width, LANES)]
    y_high = jnp.concatenate(high_tiles, axis=0)
    c = dot(jnp.concatenate([y_high] + low_tiles, axis=0), high_ref[...], ((1,), (1,)))
    c = c[: y_high.shape[0]] + c[y_high.shape[0] :] + dot(y_high, low_ref[...], ((1,), (1,)))
    sums = []
    for first in range(0, cols // LANES, TILES):
        parts = [only(t - first, c[16 * t : 16 * t + 16]) for t in range(first, min(first + TILES, cols // LANES))]
        while len(parts) > 1:
            parts = [sum(parts[k : k + 2]) for k in range(0, len(parts), 2)]
        sums.append(parts[0])
    out_ref[...] = pack(sums)


def half_image(c, high_ref, low_ref, tiles):
    high = c.astype(jnp.bfloat16).astype(jnp.float32)
    low = c - high

    def spread(v):
        return jnp.concatenate(
            [only(t % TILES, v[t // TILES * 16 : t // TILES * 16 + 16]).astype(jnp.bfloat16) for t in tiles], axis=0
        )

    high = spread(high)
    count = high.shape[0]
    z = dot(jnp.concatenate([high, spread(low)], axis=0), high_ref[...], ((1,), (0,)))
    z = z[:count] + z[count:] + dot(high, low_ref[...], ((1,), (0,)))
    z_high, z_low = split(z)
    return jnp.concatenate(
        [jnp.concatenate([z_high[k : k + 16], z_low[k : k + 16], z_high[k : k + 16]], axis=0) for k in range(0, count, 16)],
        axis=1,
    )


def momentum_kernel(both, c_ref, row_ref, high_ref, low_ref, out_ref, turned_ref, held, sems):
    high, low = split(jnp.transpose(jnp.concatenate([row_ref[...]] * 3, axis=0)))
    third = lax.broadcasted_iota(jnp.int32, high.shape, 1) >= 32
    rows = jnp.where(third, low.astype(jnp.float32), high.astype(jnp.float32)).astype(jnp.bfloat16)
    turned_ref[...] = rows
    halves = half_image(unpack(c_ref[...]), high_ref, low_ref, range(out_ref.shape[1] // LANES))
    copies = []
    for n, (start, width) in enumerate(spans(out_ref.shape[1])):
        here = slice(start, start + width)
        image = dot(rows, halves[:, here], ((1,), (0,)))
        fresh = 0.9 * both[:LANES, here].astype(jnp.float32) + both[LANES:, here].astype(jnp.float32)
        held[:, here] = (fresh - image).astype(jnp.bfloat16)
        copy = pltpu.make_async_copy(held.at[:, pl.ds(start, width)], out_ref.at[:, pl.ds(start, width)], sems.at[n])
        copy.start()
        copies.append(copy)
    for copy in copies:
        copy.wait()


def update_kernel(entries, core, total_ref, squares_ref, row_ref, high_ref, low_ref, *refs):
    out_ref, held, sems = refs[-3:]

    @pl.when(lax.axis_index("tp") % 2 == core)
    def _():
        rows = row_ref[...]
        c = unpack(total_ref[...])
        squares = jnp.sum(squares_ref[...])
        scale = lax.rsqrt(jnp.full((LANES, LANES), squares, jnp.float32) * (1.0 / entries) + 1e-06)
        first = WRITES[0][1]
        halves = [
            half_image(c, high_ref, low_ref, range(first // LANES)),
            half_image(c, high_ref, low_ref, range(first // LANES, out_ref.shape[1] // LANES)),
        ]
        copies = []
        for n, (start, width) in enumerate(WRITES):
            here = slice(start, start + width)
            half = halves[0] if n == 0 else halves[1][:, start - first : start - first + width]
            image = dot(rows, half, ((1,), (0,)))
            held[:, here] = image * jnp.concatenate([scale] * (width // LANES), axis=1)
            copy = pltpu.make_async_copy(held.at[:, pl.ds(start, width)], out_ref.at[:, pl.ds(start, width)], sems.at[n])
            copy.start()
            copies.append(copy)
        for copy in copies:
            copy.wait()


VMEM = pl.BlockSpec(memory_space=pltpu.VMEM)
ANY = pl.BlockSpec(memory_space=pl.ANY)
PARAMS = pltpu.CompilerParams(vmem_limit_bytes=VMEM_BYTES)


def hbm(x):
    return pltpu.with_memory_space_constraint(x, pltpu.HBM)


def forward(freq_rows, freq_cols, m, g):
    rows, cols = m.shape
    return pl.pallas_call(
        forward_kernel,
        out_shape=[
            jax.ShapeDtypeStruct((packed_rows(cols), LANES), jnp.float32),
            pltpu.VMEM((16, LANES), jnp.float32),
            pltpu.VMEM((LANES, LANES), jnp.bfloat16),
            pltpu.VMEM((LANES, LANES), jnp.bfloat16),
            pltpu.VMEM((2 * rows, cols), jnp.bfloat16),
        ],
        in_specs=[ANY] * 4,
        out_specs=[VMEM] * 5,
        scratch_shapes=[
            pltpu.SMEM((KEEP,), jnp.int32),
            pltpu.SMEM((KEEP,), jnp.int32),
            pltpu.SemaphoreType.DMA((2,)),
            pltpu.SemaphoreType.DMA((len(READS), 2)),
        ],
        compiler_params=PARAMS,
        cost_estimate=pl.CostEstimate(flops=2 * 48 * rows * cols, bytes_accessed=4 * rows * cols, transcendentals=0),
        name="forward",
    )(hbm(freq_rows), hbm(freq_cols), hbm(m), hbm(g))


def momentum_left(both, coeffs, row, high, low):
    rows, cols = both.shape[0] // 2, both.shape[1]
    n = len(spans(cols))
    return pl.pallas_call(
        momentum_kernel,
        out_shape=[jax.ShapeDtypeStruct((rows, cols), jnp.bfloat16), pltpu.VMEM((rows, 48), jnp.bfloat16)],
        in_specs=[VMEM] * 5,
        out_specs=[ANY, VMEM],
        scratch_shapes=[pltpu.VMEM((rows, cols), jnp.bfloat16), pltpu.SemaphoreType.DMA((len(spans(cols)),))],
        compiler_params=PARAMS,
        cost_estimate=pl.CostEstimate(flops=2 * 48 * rows * cols, bytes_accessed=2 * rows * cols, transcendentals=0),
        name="momentum",
    )(both, coeffs, row, high, low)


def updated(core, total, squares, row, high, low, cols, entries, before=None):
    rows = row.shape[0]
    given = [total, squares, row, high, low] + ([] if before is None else [before])
    return pl.pallas_call(
        functools.partial(update_kernel, entries, core),
        out_shape=jax.ShapeDtypeStruct((rows, cols), jnp.float32),
        in_specs=[VMEM] * 5 + [ANY] * (len(given) - 5),
        out_specs=ANY,
        input_output_aliases={} if before is None else {5: 0},
        scratch_shapes=[pltpu.VMEM((rows, cols), jnp.float32), pltpu.SemaphoreType.DMA((len(WRITES),))],
        compiler_params=PARAMS,
        cost_estimate=pl.CostEstimate(flops=2 * 48 * rows * cols, bytes_accessed=4 * rows * cols, transcendentals=0),
        name="update",
    )(*given)


def moved(v, partner):
    pairs = []
    for d in range(256):
        z, y, x, near, core = d // 32, d // 8 % 4, d // 4 % 2, d // 2 % 2, d % 2
        z, y, x, near, core = partner(z, y, x, near, core)
        pairs.append((d, (((z * 4 + y) * 2 + x) * 2 + near) * 2 + core))
    return lax.ppermute(v, ("rep", "tp"), pairs)


def replica(dz, dy, dx):
    def partner(z, y, x, near, core):
        if core == 0:
            return (z ^ 1, y, x, near, core) if dy else (z, y ^ 1, x, near, core)
        return z ^ dz, y ^ dy, x ^ dx, near, core

    return partner


def other_core(z, y, x, near, core):
    return z, y, x, near, 1 - core


def next_chip(z, y, x, near, core):
    return z, y, x, 1 - near, core


def four_way(v, a, b):
    both = tuple(i ^ j for i, j in zip(a, b))
    return (v + moved(v, replica(*a))) + (moved(v, replica(*b)) + moved(v, replica(*both)))


def body(momentum, grad, freq_rows, freq_cols):
    m, g = momentum[0], grad[0]
    rows, cols = m.shape
    tp = lax.axis_size("tp")
    core = lax.axis_index("tp") % 2
    own, row, high, low, both = forward(freq_rows, freq_cols, m, g)
    count = own.shape[0]
    other = moved(own, other_core)
    pair = jnp.concatenate([jnp.where(core == 1, other, own), jnp.where(core == 1, own, other)], axis=0)
    pair = four_way(pair, (0, 1, 0), (0, 2, 0))
    pair = four_way(pair, (1, 0, 0), (3, 0, 0))
    pair = pair + moved(pair, replica(6, 0, 0))
    kept, turned = momentum_left(both, own, row, high, low)
    other, kept, turned = lax.optimization_barrier((moved(pair, replica(0, 0, 1)), kept, turned))
    pair = pair + other
    squares = pair * pair
    squares = sum(squares[k : k + KEEP] for k in range(0, 2 * count, KEEP))
    squares = squares + moved(squares, next_chip)
    entries = float(rows * cols * tp)
    sent = moved(jnp.concatenate([pair[:count], squares], axis=0), other_core)
    update = updated(1, pair[count:], squares, turned, high, low, cols, entries)
    update = updated(0, sent[:count], sent[count:], turned, high, low, cols, entries, update)
    return kept[None], update


def solution(mesh):
    placed = (P("rep", None, "tp"), P("rep", None, "tp"), P(), P())
    return jax.shard_map(
        body,
        mesh=mesh,
        in_specs=placed,
        out_specs=(P("rep", None, "tp"), P(None, "tp")),
        check_vma=False,
    )
```

```python
import functools
import math

import jax
import jax.numpy as jnp
from jax import lax
from jax.experimental import pallas as pl
from jax.experimental.pallas import tpu as pltpu
from jax.sharding import PartitionSpec as P

BLOCK = 64
KEEP = 8
LANES = 128
SPAN = 1024
VMEM_BYTES = 16 * 1024 * 1024
TILES = SPAN // LANES
WRITES = [(0, 512), (512, 1024), (1536, 1920)]
READS = [(0, 2048), (2048, 1408)]


def spans(cols):
    return [(start, min(SPAN, cols - start)) for start in range(0, cols, SPAN)]


def basis_tiles(fr_ref, fc_ref):
    row = lax.broadcasted_iota(jnp.int32, (2 * KEEP, LANES), 0)
    point = lax.broadcasted_iota(jnp.int32, (2 * KEEP, LANES), 1) & (BLOCK - 1)
    freq = jnp.zeros((2 * KEEP, LANES), jnp.int32)
    for k in range(KEEP):
        freq = jnp.where(row == k, fr_ref[k], freq)
        freq = jnp.where(row == KEEP + k, fc_ref[k], freq)
    turn = ((2 * point + 1) * freq) & (4 * BLOCK - 1)
    turn = jnp.minimum(turn, 4 * BLOCK - turn)
    x = (BLOCK - turn).astype(jnp.float32) * (math.pi / (2 * BLOCK))
    y = x * x
    series = jnp.full_like(x, 1.0 / math.factorial(13))
    for n in (11, 9, 7, 5, 3, 1):
        series = 1.0 / math.factorial(n) - series * y
    scale = jnp.where(freq == 0, math.sqrt(1.0 / BLOCK), math.sqrt(2.0 / BLOCK))
    return x * series * scale


def split(v):
    high = v.astype(jnp.bfloat16)
    return high, (v - high.astype(jnp.float32)).astype(jnp.bfloat16)


def two_blocks(tile):
    lane = lax.broadcasted_iota(jnp.int32, (KEEP, LANES), 1)
    return jnp.concatenate([jnp.where(lane < BLOCK, tile, 0.0), jnp.where(lane >= BLOCK, tile, 0.0)], axis=0)


def only(t, v):
    lane = lax.broadcasted_iota(jnp.int32, v.shape, 1)
    return jnp.where((lane >> 4) == t, v, 0.0)


def dot(a, b, dims):
    return lax.dot_general(a, b, (dims, ((), ())), preferred_element_type=jnp.float32)


def packed_rows(cols):
    whole, left = divmod(cols, SPAN)
    assert 0 < left <= SPAN // 2
    return 16 * whole + 8


def pack(spans16):
    last = spans16[-1]
    return jnp.concatenate(spans16[:-1] + [last[:8] + pltpu.roll(last[8:], LANES // 2, 1)], axis=0)


def unpack(rows):
    last = rows[-8:]
    return jnp.concatenate([rows, pltpu.roll(last, LANES // 2, 1)], axis=0)


def forward_kernel(
    fr_ref, fc_ref, m_ref, g_ref, out_ref, row_ref, high_ref, low_ref, both, fr_smem, fc_smem, fsems, sems
):
    cols = m_ref.shape[1]
    freqs = [
        pltpu.make_async_copy(src, dst, fsems.at[k]) for k, (src, dst) in enumerate(((fr_ref, fr_smem), (fc_ref, fc_smem)))
    ]
    for copy in freqs:
        copy.start()
    copies = []
    for n, (start, width) in enumerate(READS):
        for k, src in enumerate((m_ref, g_ref)):
            copy = pltpu.make_async_copy(
                src.at[:, pl.ds(start, width)], both.at[pl.ds(LANES * k, LANES), pl.ds(start, width)], sems.at[n, k]
            )
            copy.start()
            copies.append(copy)
    for copy in freqs:
        copy.wait()
    tiles = basis_tiles(fr_smem, fc_smem)
    rows = two_blocks(tiles[:KEEP])
    row_ref[...] = rows
    high, low = split(jnp.concatenate([0.9 * rows, rows], axis=1))
    lhs = jnp.concatenate([high, low], axis=0)
    high, low = split(two_blocks(tiles[KEEP:]))
    high_ref[...] = jnp.concatenate([high] * TILES, axis=0)
    low_ref[...] = jnp.concatenate([low] * TILES, axis=0)
    high_tiles, low_tiles = [], []
    for n, (start, width) in enumerate(READS):
        copies[2 * n].wait()
        copies[2 * n + 1].wait()
        y = dot(lhs, both[:, start : start + width], ((1,), (0,)))
        high, low = split(y[:16] + y[16:])
        high_tiles += [high[:, k : k + LANES] for k in range(0, width, LANES)]
        low_tiles += [low[:, k : k + LANES] for k in range(0, width, LANES)]
    y_high = jnp.concatenate(high_tiles, axis=0)
    c = dot(jnp.concatenate([y_high] + low_tiles, axis=0), high_ref[...], ((1,), (1,)))
    c = c[: y_high.shape[0]] + c[y_high.shape[0] :] + dot(y_high, low_ref[...], ((1,), (1,)))
    sums = []
    for first in range(0, cols // LANES, TILES):
        parts = [only(t - first, c[16 * t : 16 * t + 16]) for t in range(first, min(first + TILES, cols // LANES))]
        while len(parts) > 1:
            parts = [sum(parts[k : k + 2]) for k in range(0, len(parts), 2)]
        sums.append(parts[0])
    out_ref[...] = pack(sums)


def half_image(c, high_ref, low_ref, tiles):
    high = c.astype(jnp.bfloat16).astype(jnp.float32)
    low = c - high

    def spread(v):
        return jnp.concatenate(
            [only(t % TILES, v[t // TILES * 16 : t // TILES * 16 + 16]).astype(jnp.bfloat16) for t in tiles], axis=0
        )

    high = spread(high)
    count = high.shape[0]
    z = dot(jnp.concatenate([high, spread(low)], axis=0), high_ref[...], ((1,), (0,)))
    z = z[:count] + z[count:] + dot(high, low_ref[...], ((1,), (0,)))
    z_high, z_low = split(z)
    return jnp.concatenate(
        [jnp.concatenate([z_high[k : k + 16], z_low[k : k + 16], z_high[k : k + 16]], axis=0) for k in range(0, count, 16)],
        axis=1,
    )


def momentum_kernel(both, c_ref, row_ref, high_ref, low_ref, out_ref, turned_ref, held, sems):
    high, low = split(jnp.transpose(jnp.concatenate([row_ref[...]] * 3, axis=0)))
    third = lax.broadcasted_iota(jnp.int32, high.shape, 1) >= 32
    rows = jnp.where(third, low.astype(jnp.float32), high.astype(jnp.float32)).astype(jnp.bfloat16)
    turned_ref[...] = rows
    halves = half_image(unpack(c_ref[...]), high_ref, low_ref, range(out_ref.shape[1] // LANES))
    copies = []
    for n, (start, width) in enumerate(spans(out_ref.shape[1])):
        here = slice(start, start + width)
        image = dot(rows, halves[:, here], ((1,), (0,)))
        fresh = 0.9 * both[:LANES, here].astype(jnp.float32) + both[LANES:, here].astype(jnp.float32)
        held[:, here] = (fresh - image).astype(jnp.bfloat16)
        copy = pltpu.make_async_copy(held.at[:, pl.ds(start, width)], out_ref.at[:, pl.ds(start, width)], sems.at[n])
        copy.start()
        copies.append(copy)
    for copy in copies:
        copy.wait()


def update_kernel(entries, core, total_ref, squares_ref, row_ref, high_ref, low_ref, *refs):
    out_ref, held, sems = refs[-3:]

    @pl.when(lax.axis_index("tp") % 2 == core)
    def _():
        rows = row_ref[...]
        c = unpack(total_ref[...])
        squares = jnp.sum(squares_ref[...])
        scale = lax.rsqrt(jnp.full((LANES, LANES), squares, jnp.float32) * (1.0 / entries) + 1e-06)
        first = WRITES[0][1]
        halves = [
            half_image(c, high_ref, low_ref, range(first // LANES)),
            half_image(c, high_ref, low_ref, range(first // LANES, out_ref.shape[1] // LANES)),
        ]
        copies = []
        for n, (start, width) in enumerate(WRITES):
            here = slice(start, start + width)
            half = halves[0] if n == 0 else halves[1][:, start - first : start - first + width]
            image = dot(rows, half, ((1,), (0,)))
            held[:, here] = image * jnp.concatenate([scale] * (width // LANES), axis=1)
            copy = pltpu.make_async_copy(held.at[:, pl.ds(start, width)], out_ref.at[:, pl.ds(start, width)], sems.at[n])
            copy.start()
            copies.append(copy)
        for copy in copies:
            copy.wait()


VMEM = pl.BlockSpec(memory_space=pltpu.VMEM)
ANY = pl.BlockSpec(memory_space=pl.ANY)
PARAMS = pltpu.CompilerParams(vmem_limit_bytes=VMEM_BYTES)


def hbm(x):
    return pltpu.with_memory_space_constraint(x, pltpu.HBM)


def forward(freq_rows, freq_cols, m, g):
    rows, cols = m.shape
    return pl.pallas_call(
        forward_kernel,
        out_shape=[
            jax.ShapeDtypeStruct((packed_rows(cols), LANES), jnp.float32),
            pltpu.VMEM((16, LANES), jnp.float32),
            pltpu.VMEM((LANES, LANES), jnp.bfloat16),
            pltpu.VMEM((LANES, LANES), jnp.bfloat16),
            pltpu.VMEM((2 * rows, cols), jnp.bfloat16),
        ],
        in_specs=[ANY] * 4,
        out_specs=[VMEM] * 5,
        scratch_shapes=[
            pltpu.SMEM((KEEP,), jnp.int32),
            pltpu.SMEM((KEEP,), jnp.int32),
            pltpu.SemaphoreType.DMA((2,)),
            pltpu.SemaphoreType.DMA((len(READS), 2)),
        ],
        compiler_params=PARAMS,
        cost_estimate=pl.CostEstimate(flops=2 * 48 * rows * cols, bytes_accessed=4 * rows * cols, transcendentals=0),
        name="forward",
    )(hbm(freq_rows), hbm(freq_cols), hbm(m), hbm(g))


def momentum_left(both, coeffs, row, high, low):
    rows, cols = both.shape[0] // 2, both.shape[1]
    n = len(spans(cols))
    return pl.pallas_call(
        momentum_kernel,
        out_shape=[jax.ShapeDtypeStruct((rows, cols), jnp.bfloat16), pltpu.VMEM((rows, 48), jnp.bfloat16)],
        in_specs=[VMEM] * 5,
        out_specs=[ANY, VMEM],
        scratch_shapes=[pltpu.VMEM((rows, cols), jnp.bfloat16), pltpu.SemaphoreType.DMA((len(spans(cols)),))],
        compiler_params=PARAMS,
        cost_estimate=pl.CostEstimate(flops=2 * 48 * rows * cols, bytes_accessed=2 * rows * cols, transcendentals=0),
        name="momentum",
    )(both, coeffs, row, high, low)


def updated(core, total, squares, row, high, low, cols, entries, before=None):
    rows = row.shape[0]
    given = [total, squares, row, high, low] + ([] if before is None else [before])
    return pl.pallas_call(
        functools.partial(update_kernel, entries, core),
        out_shape=jax.ShapeDtypeStruct((rows, cols), jnp.float32),
        in_specs=[VMEM] * 5 + [ANY] * (len(given) - 5),
        out_specs=ANY,
        input_output_aliases={} if before is None else {5: 0},
        scratch_shapes=[pltpu.VMEM((rows, cols), jnp.float32), pltpu.SemaphoreType.DMA((len(WRITES),))],
        compiler_params=PARAMS,
        cost_estimate=pl.CostEstimate(flops=2 * 48 * rows * cols, bytes_accessed=4 * rows * cols, transcendentals=0),
        name="update",
    )(*given)


def moved(v, partner):
    pairs = []
    for d in range(256):
        z, y, x, near, core = d // 32, d // 8 % 4, d // 4 % 2, d // 2 % 2, d % 2
        z, y, x, near, core = partner(z, y, x, near, core)
        pairs.append((d, (((z * 4 + y) * 2 + x) * 2 + near) * 2 + core))
    return lax.ppermute(v, ("rep", "tp"), pairs)


def replica(dz, dy, dx):
    def partner(z, y, x, near, core):
        if core == 0:
            return (z ^ 1, y, x, near, core) if dy else (z, y ^ 1, x, near, core)
        return z ^ dz, y ^ dy, x ^ dx, near, core

    return partner


def other_core(z, y, x, near, core):
    return z, y, x, near, 1 - core


def next_chip(z, y, x, near, core):
    return z, y, x, 1 - near, core


def four_way(v, a, b):
    both = tuple(i ^ j for i, j in zip(a, b))
    return (v + moved(v, replica(*a))) + (moved(v, replica(*b)) + moved(v, replica(*both)))


def ring(dx, dnear):
    def partner(z, y, x, near, core):
        if core == 0:
            return z, y ^ 1, x, near, core
        return z, y, x ^ dx, near ^ dnear, core

    return partner


def body(momentum, grad, freq_rows, freq_cols):
    m, g = momentum[0], grad[0]
    rows, cols = m.shape
    tp = lax.axis_size("tp")
    core = lax.axis_index("tp") % 2
    own, row, high, low, both = forward(freq_rows, freq_cols, m, g)
    count = own.shape[0]
    other = moved(own, other_core)
    pair = jnp.concatenate([jnp.where(core == 1, other, own), jnp.where(core == 1, own, other)], axis=0)
    pair = four_way(pair, (0, 1, 0), (0, 2, 0))
    pair = four_way(pair, (1, 0, 0), (3, 0, 0))
    pair = pair + moved(pair, replica(6, 0, 0))
    kept, turned = momentum_left(both, own, row, high, low)
    got = {}
    for dx, dnear in [(0, 1), (1, 0), (1, 1)]:
        got[dx, dnear] = moved(pair, ring(dx, dnear))
    got, kept, turned = lax.optimization_barrier((got, kept, turned))
    pair = pair + got[1, 0]
    beside = got[0, 1] + got[1, 1]
    squares = pair * pair + beside * beside
    squares = sum(squares[k : k + KEEP] for k in range(0, 2 * count, KEEP))
    entries = float(rows * cols * tp)
    sent = moved(jnp.concatenate([pair[:count], squares], axis=0), other_core)
    update = updated(1, pair[count:], squares, turned, high, low, cols, entries)
    update = updated(0, sent[:count], sent[count:], turned, high, low, cols, entries, update)
    return kept[None], update


def solution(mesh):
    placed = (P("rep", None, "tp"), P("rep", None, "tp"), P(), P())
    return jax.shard_map(
        body,
        mesh=mesh,
        in_specs=placed,
        out_specs=(P("rep", None, "tp"), P(None, "tp")),
        check_vma=False,
    )
```

```python
import functools
import math

import jax
import jax.numpy as jnp
from jax import lax
from jax.experimental import pallas as pl
from jax.experimental.pallas import tpu as pltpu
from jax.sharding import PartitionSpec as P

BLOCK = 64
KEEP = 8
LANES = 128
SPAN = 1024
VMEM_BYTES = 16 * 1024 * 1024
TILES = SPAN // LANES
WRITES = [(0, 512), (512, 1024), (1536, 1920)]
READS = [(0, 1536), (1536, 1920)]


def spans(cols):
    return [(start, min(SPAN, cols - start)) for start in range(0, cols, SPAN)]


def basis_tiles(fr_ref, fc_ref):
    row = lax.broadcasted_iota(jnp.int32, (2 * KEEP, LANES), 0)
    point = lax.broadcasted_iota(jnp.int32, (2 * KEEP, LANES), 1) & (BLOCK - 1)
    freq = jnp.zeros((2 * KEEP, LANES), jnp.int32)
    for k in range(KEEP):
        freq = jnp.where(row == k, fr_ref[k], freq)
        freq = jnp.where(row == KEEP + k, fc_ref[k], freq)
    turn = ((2 * point + 1) * freq) & (4 * BLOCK - 1)
    turn = jnp.minimum(turn, 4 * BLOCK - turn)
    x = (BLOCK - turn).astype(jnp.float32) * (math.pi / (2 * BLOCK))
    y = x * x
    series = jnp.full_like(x, 1.0 / math.factorial(13))
    for n in (11, 9, 7, 5, 3, 1):
        series = 1.0 / math.factorial(n) - series * y
    scale = jnp.where(freq == 0, math.sqrt(1.0 / BLOCK), math.sqrt(2.0 / BLOCK))
    return x * series * scale


def split(v):
    high = v.astype(jnp.bfloat16)
    return high, (v - high.astype(jnp.float32)).astype(jnp.bfloat16)


def two_blocks(tile):
    lane = lax.broadcasted_iota(jnp.int32, (KEEP, LANES), 1)
    return jnp.concatenate([jnp.where(lane < BLOCK, tile, 0.0), jnp.where(lane >= BLOCK, tile, 0.0)], axis=0)


def only(t, v):
    lane = lax.broadcasted_iota(jnp.int32, v.shape, 1)
    return jnp.where((lane >> 4) == t, v, 0.0)


def dot(a, b, dims):
    return lax.dot_general(a, b, (dims, ((), ())), preferred_element_type=jnp.float32)


def packed_rows(cols):
    whole, left = divmod(cols, SPAN)
    assert 0 < left <= SPAN // 2
    return 16 * whole + 8


def pack(spans16):
    last = spans16[-1]
    return jnp.concatenate(spans16[:-1] + [last[:8] + pltpu.roll(last[8:], LANES // 2, 1)], axis=0)


def unpack(rows):
    last = rows[-8:]
    return jnp.concatenate([rows, pltpu.roll(last, LANES // 2, 1)], axis=0)


def forward_kernel(
    fr_ref, fc_ref, m_ref, g_ref, out_ref, row_ref, high_ref, low_ref, both, fr_smem, fc_smem, fsems, sems
):
    cols = m_ref.shape[1]
    freqs = [
        pltpu.make_async_copy(src, dst, fsems.at[k]) for k, (src, dst) in enumerate(((fr_ref, fr_smem), (fc_ref, fc_smem)))
    ]
    for copy in freqs:
        copy.start()
    copies = []
    for n, (start, width) in enumerate(READS):
        for k, src in enumerate((m_ref, g_ref)):
            copy = pltpu.make_async_copy(
                src.at[:, pl.ds(start, width)], both.at[pl.ds(LANES * k, LANES), pl.ds(start, width)], sems.at[n, k]
            )
            copy.start()
            copies.append(copy)
    for copy in freqs:
        copy.wait()
    tiles = basis_tiles(fr_smem, fc_smem)
    rows = two_blocks(tiles[:KEEP])
    row_ref[...] = rows
    high, low = split(jnp.concatenate([0.9 * rows, rows], axis=1))
    lhs = jnp.concatenate([high, low], axis=0)
    high, low = split(two_blocks(tiles[KEEP:]))
    high_ref[...] = jnp.concatenate([high] * TILES, axis=0)
    low_ref[...] = jnp.concatenate([low] * TILES, axis=0)
    high_tiles, low_tiles = [], []
    for n, (start, width) in enumerate(READS):
        copies[2 * n].wait()
        copies[2 * n + 1].wait()
        y = dot(lhs, both[:, start : start + width], ((1,), (0,)))
        high, low = split(y[:16] + y[16:])
        high_tiles += [high[:, k : k + LANES] for k in range(0, width, LANES)]
        low_tiles += [low[:, k : k + LANES] for k in range(0, width, LANES)]
    y_high = jnp.concatenate(high_tiles, axis=0)
    y_both = jnp.concatenate([y_high, jnp.concatenate(low_tiles, axis=0)], axis=1)
    c = dot(y_both, jnp.concatenate([high_ref[...]] * 2, axis=1), ((1,), (1,)))
    c = c + dot(y_high, low_ref[...], ((1,), (1,)))
    sums = []
    for first in range(0, cols // LANES, TILES):
        parts = [only(t - first, c[16 * t : 16 * t + 16]) for t in range(first, min(first + TILES, cols // LANES))]
        while len(parts) > 1:
            parts = [sum(parts[k : k + 2]) for k in range(0, len(parts), 2)]
        sums.append(parts[0])
    out_ref[...] = pack(sums)


def half_image(c, high_ref, low_ref, tiles):
    high = c.astype(jnp.bfloat16).astype(jnp.float32)
    low = c - high

    def spread(v):
        return jnp.concatenate(
            [only(t % TILES, v[t // TILES * 16 : t // TILES * 16 + 16]).astype(jnp.bfloat16) for t in tiles], axis=0
        )

    high = spread(high)
    count = high.shape[0]
    z = dot(jnp.concatenate([high, spread(low)], axis=0), high_ref[...], ((1,), (0,)))
    z = z[:count] + z[count:] + dot(high, low_ref[...], ((1,), (0,)))
    z_high, z_low = split(z)
    return jnp.concatenate(
        [jnp.concatenate([z_high[k : k + 16], z_low[k : k + 16], z_high[k : k + 16]], axis=0) for k in range(0, count, 16)],
        axis=1,
    )


def momentum_kernel(both, c_ref, row_ref, high_ref, low_ref, out_ref, turned_ref, held, sems):
    high, low = split(jnp.transpose(jnp.concatenate([row_ref[...]] * 3, axis=0)))
    third = lax.broadcasted_iota(jnp.int32, high.shape, 1) >= 32
    rows = jnp.where(third, low.astype(jnp.float32), high.astype(jnp.float32)).astype(jnp.bfloat16)
    turned_ref[...] = rows
    halves = half_image(unpack(c_ref[...]), high_ref, low_ref, range(out_ref.shape[1] // LANES))
    copies = []
    for n, (start, width) in enumerate(spans(out_ref.shape[1])):
        here = slice(start, start + width)
        image = dot(rows, halves[:, here], ((1,), (0,)))
        fresh = 0.9 * both[:LANES, here].astype(jnp.float32) + both[LANES:, here].astype(jnp.float32)
        held[:, here] = (fresh - image).astype(jnp.bfloat16)
        copy = pltpu.make_async_copy(held.at[:, pl.ds(start, width)], out_ref.at[:, pl.ds(start, width)], sems.at[n])
        copy.start()
        copies.append(copy)
    for copy in copies:
        copy.wait()


def update_kernel(entries, core, total_ref, squares_ref, row_ref, high_ref, low_ref, *refs):
    out_ref, held, sems = refs[-3:]

    @pl.when(lax.axis_index("tp") % 2 == core)
    def _():
        rows = row_ref[...]
        c = unpack(total_ref[...])
        squares = jnp.sum(squares_ref[...])
        scale = lax.rsqrt(jnp.full((LANES, LANES), squares, jnp.float32) * (1.0 / entries) + 1e-06)
        first = WRITES[0][1]
        halves = [
            half_image(c, high_ref, low_ref, range(first // LANES)),
            half_image(c, high_ref, low_ref, range(first // LANES, out_ref.shape[1] // LANES)),
        ]
        copies = []
        for n, (start, width) in enumerate(WRITES):
            here = slice(start, start + width)
            half = halves[0] if n == 0 else halves[1][:, start - first : start - first + width]
            image = dot(rows, half, ((1,), (0,)))
            held[:, here] = image * jnp.concatenate([scale] * (width // LANES), axis=1)
            copy = pltpu.make_async_copy(held.at[:, pl.ds(start, width)], out_ref.at[:, pl.ds(start, width)], sems.at[n])
            copy.start()
            copies.append(copy)
        for copy in copies:
            copy.wait()


VMEM = pl.BlockSpec(memory_space=pltpu.VMEM)
ANY = pl.BlockSpec(memory_space=pl.ANY)
PARAMS = pltpu.CompilerParams(vmem_limit_bytes=VMEM_BYTES)


def hbm(x):
    return pltpu.with_memory_space_constraint(x, pltpu.HBM)


def forward(freq_rows, freq_cols, m, g):
    rows, cols = m.shape
    return pl.pallas_call(
        forward_kernel,
        out_shape=[
            jax.ShapeDtypeStruct((packed_rows(cols), LANES), jnp.float32),
            pltpu.VMEM((16, LANES), jnp.float32),
            pltpu.VMEM((LANES, LANES), jnp.bfloat16),
            pltpu.VMEM((LANES, LANES), jnp.bfloat16),
            pltpu.VMEM((2 * rows, cols), jnp.bfloat16),
        ],
        in_specs=[ANY] * 4,
        out_specs=[VMEM] * 5,
        scratch_shapes=[
            pltpu.SMEM((KEEP,), jnp.int32),
            pltpu.SMEM((KEEP,), jnp.int32),
            pltpu.SemaphoreType.DMA((2,)),
            pltpu.SemaphoreType.DMA((len(READS), 2)),
        ],
        compiler_params=PARAMS,
        cost_estimate=pl.CostEstimate(flops=2 * 48 * rows * cols, bytes_accessed=4 * rows * cols, transcendentals=0),
        name="forward",
    )(hbm(freq_rows), hbm(freq_cols), hbm(m), hbm(g))


def momentum_left(both, coeffs, row, high, low):
    rows, cols = both.shape[0] // 2, both.shape[1]
    n = len(spans(cols))
    return pl.pallas_call(
        momentum_kernel,
        out_shape=[jax.ShapeDtypeStruct((rows, cols), jnp.bfloat16), pltpu.VMEM((rows, 48), jnp.bfloat16)],
        in_specs=[VMEM] * 5,
        out_specs=[ANY, VMEM],
        scratch_shapes=[pltpu.VMEM((rows, cols), jnp.bfloat16), pltpu.SemaphoreType.DMA((len(spans(cols)),))],
        compiler_params=PARAMS,
        cost_estimate=pl.CostEstimate(flops=2 * 48 * rows * cols, bytes_accessed=2 * rows * cols, transcendentals=0),
        name="momentum",
    )(both, coeffs, row, high, low)


def updated(core, total, squares, row, high, low, cols, entries, before=None):
    rows = row.shape[0]
    given = [total, squares, row, high, low] + ([] if before is None else [before])
    return pl.pallas_call(
        functools.partial(update_kernel, entries, core),
        out_shape=jax.ShapeDtypeStruct((rows, cols), jnp.float32),
        in_specs=[VMEM] * 5 + [ANY] * (len(given) - 5),
        out_specs=ANY,
        input_output_aliases={} if before is None else {5: 0},
        scratch_shapes=[pltpu.VMEM((rows, cols), jnp.float32), pltpu.SemaphoreType.DMA((len(WRITES),))],
        compiler_params=PARAMS,
        cost_estimate=pl.CostEstimate(flops=2 * 48 * rows * cols, bytes_accessed=4 * rows * cols, transcendentals=0),
        name="update",
    )(*given)


def moved(v, partner):
    pairs = []
    for d in range(256):
        z, y, x, near, core = d // 32, d // 8 % 4, d // 4 % 2, d // 2 % 2, d % 2
        z, y, x, near, core = partner(z, y, x, near, core)
        pairs.append((d, (((z * 4 + y) * 2 + x) * 2 + near) * 2 + core))
    return lax.ppermute(v, ("rep", "tp"), pairs)


def replica(dz, dy, dx):
    def partner(z, y, x, near, core):
        if core == 0:
            return (z ^ 1, y, x, near, core) if dy else (z, y ^ 1, x, near, core)
        return z ^ dz, y ^ dy, x ^ dx, near, core

    return partner


def other_core(z, y, x, near, core):
    return z, y, x, near, 1 - core


def next_chip(z, y, x, near, core):
    return z, y, x, 1 - near, core


def four_way(v, a, b):
    both = tuple(i ^ j for i, j in zip(a, b))
    return (v + moved(v, replica(*a))) + (moved(v, replica(*b)) + moved(v, replica(*both)))


def body(momentum, grad, freq_rows, freq_cols):
    m, g = momentum[0], grad[0]
    rows, cols = m.shape
    tp = lax.axis_size("tp")
    core = lax.axis_index("tp") % 2
    own, row, high, low, both = forward(freq_rows, freq_cols, m, g)
    count = own.shape[0]
    other = moved(own, other_core)
    pair = jnp.concatenate([jnp.where(core == 1, other, own), jnp.where(core == 1, own, other)], axis=0)
    pair = four_way(pair, (0, 1, 0), (0, 2, 0))
    pair = four_way(pair, (1, 0, 0), (3, 0, 0))
    pair = pair + moved(pair, replica(6, 0, 0))
    kept, turned = momentum_left(both, own, row, high, low)
    other, kept, turned = lax.optimization_barrier((moved(pair, replica(0, 0, 1)), kept, turned))
    pair = pair + other
    squares = pair * pair
    squares = sum(squares[k : k + KEEP] for k in range(0, 2 * count, KEEP))
    squares = squares + moved(squares, next_chip)
    entries = float(rows * cols * tp)
    sent = moved(jnp.concatenate([pair[:count], squares], axis=0), other_core)
    update = updated(1, pair[count:], squares, turned, high, low, cols, entries)
    update = updated(0, sent[:count], sent[count:], turned, high, low, cols, entries, update)
    return kept[None], update


def solution(mesh):
    placed = (P("rep", None, "tp"), P("rep", None, "tp"), P(), P())
    return jax.shard_map(
        body,
        mesh=mesh,
        in_specs=placed,
        out_specs=(P("rep", None, "tp"), P(None, "tp")),
        check_vma=False,
    )
```

```python
import functools
import math

import jax
import jax.numpy as jnp
from jax import lax
from jax.experimental import pallas as pl
from jax.experimental.pallas import tpu as pltpu
from jax.sharding import PartitionSpec as P

BLOCK = 64
KEEP = 8
LANES = 128
SPAN = 1024
VMEM_BYTES = 16 * 1024 * 1024
TILES = SPAN // LANES
WRITES = [(0, 512), (512, 1024), (1536, 1920)]
READS = [(0, 1536), (1536, 1920)]


def spans(cols):
    return [(start, min(SPAN, cols - start)) for start in range(0, cols, SPAN)]


def basis_tiles(fr_ref, fc_ref):
    row = lax.broadcasted_iota(jnp.int32, (2 * KEEP, LANES), 0)
    point = lax.broadcasted_iota(jnp.int32, (2 * KEEP, LANES), 1) & (BLOCK - 1)
    freq = jnp.zeros((2 * KEEP, LANES), jnp.int32)
    for k in range(KEEP):
        freq = jnp.where(row == k, fr_ref[k], freq)
        freq = jnp.where(row == KEEP + k, fc_ref[k], freq)
    turn = ((2 * point + 1) * freq) & (4 * BLOCK - 1)
    turn = jnp.minimum(turn, 4 * BLOCK - turn)
    x = (BLOCK - turn).astype(jnp.float32) * (math.pi / (2 * BLOCK))
    y = x * x
    series = jnp.full_like(x, 1.0 / math.factorial(13))
    for n in (11, 9, 7, 5, 3, 1):
        series = 1.0 / math.factorial(n) - series * y
    scale = jnp.where(freq == 0, math.sqrt(1.0 / BLOCK), math.sqrt(2.0 / BLOCK))
    return x * series * scale


def split(v):
    high = v.astype(jnp.bfloat16)
    return high, (v - high.astype(jnp.float32)).astype(jnp.bfloat16)


def two_blocks(tile):
    lane = lax.broadcasted_iota(jnp.int32, (KEEP, LANES), 1)
    return jnp.concatenate([jnp.where(lane < BLOCK, tile, 0.0), jnp.where(lane >= BLOCK, tile, 0.0)], axis=0)


def only(t, v):
    lane = lax.broadcasted_iota(jnp.int32, v.shape, 1)
    return jnp.where((lane >> 4) == t, v, 0.0)


def dot(a, b, dims):
    return lax.dot_general(a, b, (dims, ((), ())), preferred_element_type=jnp.float32)


def packed_rows(cols):
    whole, left = divmod(cols, SPAN)
    assert 0 < left <= SPAN // 2
    return 16 * whole + 8


def pack(spans16):
    last = spans16[-1]
    return jnp.concatenate(spans16[:-1] + [last[:8] + pltpu.roll(last[8:], LANES // 2, 1)], axis=0)


def unpack(rows):
    last = rows[-8:]
    return jnp.concatenate([rows, pltpu.roll(last, LANES // 2, 1)], axis=0)


def forward_kernel(
    fr_ref, fc_ref, m_ref, g_ref, out_ref, row_ref, high_ref, low_ref, both, fr_smem, fc_smem, fsems, sems
):
    cols = m_ref.shape[1]
    freqs = [
        pltpu.make_async_copy(src, dst, fsems.at[k]) for k, (src, dst) in enumerate(((fr_ref, fr_smem), (fc_ref, fc_smem)))
    ]
    for copy in freqs:
        copy.start()
    copies = []
    for n, (start, width) in enumerate(READS):
        for k, src in enumerate((m_ref, g_ref)):
            copy = pltpu.make_async_copy(
                src.at[:, pl.ds(start, width)], both.at[pl.ds(LANES * k, LANES), pl.ds(start, width)], sems.at[n, k]
            )
            copy.start()
            copies.append(copy)
    for copy in freqs:
        copy.wait()
    tiles = basis_tiles(fr_smem, fc_smem)
    rows = two_blocks(tiles[:KEEP])
    row_ref[...] = rows
    high, low = split(jnp.concatenate([0.9 * rows, rows], axis=1))
    lhs = jnp.concatenate([high, low], axis=0)
    high, low = split(two_blocks(tiles[KEEP:]))
    high_ref[...] = jnp.concatenate([high] * TILES, axis=0)
    low_ref[...] = jnp.concatenate([low] * TILES, axis=0)
    high_tiles, low_tiles = [], []
    for n, (start, width) in enumerate(READS):
        copies[2 * n].wait()
        copies[2 * n + 1].wait()
        y = dot(lhs, both[:, start : start + width], ((1,), (0,)))
        high, low = split(y[:16] + y[16:])
        high_tiles += [high[:, k : k + LANES] for k in range(0, width, LANES)]
        low_tiles += [low[:, k : k + LANES] for k in range(0, width, LANES)]
    y_high = jnp.concatenate(high_tiles, axis=0)
    y_both = jnp.concatenate([y_high, jnp.concatenate(low_tiles, axis=0)], axis=1)
    c = dot(y_both, jnp.concatenate([high_ref[...]] * 2, axis=1), ((1,), (1,)))
    c = c + dot(y_high, low_ref[...], ((1,), (1,)))
    sums = []
    for first in range(0, cols // LANES, TILES):
        parts = [only(t - first, c[16 * t : 16 * t + 16]) for t in range(first, min(first + TILES, cols // LANES))]
        while len(parts) > 1:
            parts = [sum(parts[k : k + 2]) for k in range(0, len(parts), 2)]
        sums.append(parts[0])
    out_ref[...] = pack(sums)


def half_image(c, high_ref, low_ref, tiles):
    high = c.astype(jnp.bfloat16).astype(jnp.float32)
    low = c - high

    def spread(v):
        return jnp.concatenate(
            [only(t % TILES, v[t // TILES * 16 : t // TILES * 16 + 16]).astype(jnp.bfloat16) for t in tiles], axis=0
        )

    high = spread(high)
    count = high.shape[0]
    z = dot(jnp.concatenate([high, spread(low)], axis=0), high_ref[...], ((1,), (0,)))
    z = z[:count] + z[count:] + dot(high, low_ref[...], ((1,), (0,)))
    z_high, z_low = split(z)
    return jnp.concatenate(
        [jnp.concatenate([z_high[k : k + 16], z_low[k : k + 16], z_high[k : k + 16]], axis=0) for k in range(0, count, 16)],
        axis=1,
    )


def momentum_kernel(both, c_ref, row_ref, high_ref, low_ref, out_ref, turned_ref, held, sems):
    high, low = split(jnp.transpose(jnp.concatenate([row_ref[...]] * 3, axis=0)))
    third = lax.broadcasted_iota(jnp.int32, high.shape, 1) >= 32
    rows = jnp.where(third, low.astype(jnp.float32), high.astype(jnp.float32)).astype(jnp.bfloat16)
    turned_ref[...] = rows
    halves = half_image(unpack(c_ref[...]), high_ref, low_ref, range(out_ref.shape[1] // LANES))
    copies = []
    for n, (start, width) in enumerate(spans(out_ref.shape[1])):
        here = slice(start, start + width)
        image = dot(rows, halves[:, here], ((1,), (0,)))
        fresh = 0.9 * both[:LANES, here].astype(jnp.float32) + both[LANES:, here].astype(jnp.float32)
        held[:, here] = (fresh - image).astype(jnp.bfloat16)
        copy = pltpu.make_async_copy(held.at[:, pl.ds(start, width)], out_ref.at[:, pl.ds(start, width)], sems.at[n])
        copy.start()
        copies.append(copy)
    for copy in copies:
        copy.wait()


def update_kernel(entries, core, total_ref, squares_ref, row_ref, high_ref, low_ref, *refs):
    out_ref, held, sems = refs[-3:]

    @pl.when(lax.axis_index("tp") % 2 == core)
    def _():
        rows = row_ref[...]
        c = unpack(total_ref[...])
        squares = jnp.sum(squares_ref[...])
        scale = lax.rsqrt(jnp.full((LANES, LANES), squares, jnp.float32) * (1.0 / entries) + 1e-06)
        first = WRITES[0][1]
        halves = [
            half_image(c, high_ref, low_ref, range(first // LANES)),
            half_image(c, high_ref, low_ref, range(first // LANES, out_ref.shape[1] // LANES)),
        ]
        copies = []
        for n, (start, width) in enumerate(WRITES):
            here = slice(start, start + width)
            half = halves[0] if n == 0 else halves[1][:, start - first : start - first + width]
            image = dot(rows, half, ((1,), (0,)))
            held[:, here] = image * jnp.concatenate([scale] * (width // LANES), axis=1)
            copy = pltpu.make_async_copy(held.at[:, pl.ds(start, width)], out_ref.at[:, pl.ds(start, width)], sems.at[n])
            copy.start()
            copies.append(copy)
        for copy in copies:
            copy.wait()


VMEM = pl.BlockSpec(memory_space=pltpu.VMEM)
ANY = pl.BlockSpec(memory_space=pl.ANY)
PARAMS = pltpu.CompilerParams(vmem_limit_bytes=VMEM_BYTES)


def hbm(x):
    return pltpu.with_memory_space_constraint(x, pltpu.HBM)


def forward(freq_rows, freq_cols, m, g):
    rows, cols = m.shape
    return pl.pallas_call(
        forward_kernel,
        out_shape=[
            jax.ShapeDtypeStruct((packed_rows(cols), LANES), jnp.float32),
            pltpu.VMEM((16, LANES), jnp.float32),
            pltpu.VMEM((LANES, LANES), jnp.bfloat16),
            pltpu.VMEM((LANES, LANES), jnp.bfloat16),
            pltpu.VMEM((2 * rows, cols), jnp.bfloat16),
        ],
        in_specs=[ANY] * 4,
        out_specs=[VMEM] * 5,
        scratch_shapes=[
            pltpu.SMEM((KEEP,), jnp.int32),
            pltpu.SMEM((KEEP,), jnp.int32),
            pltpu.SemaphoreType.DMA((2,)),
            pltpu.SemaphoreType.DMA((len(READS), 2)),
        ],
        compiler_params=PARAMS,
        cost_estimate=pl.CostEstimate(flops=2 * 48 * rows * cols, bytes_accessed=4 * rows * cols, transcendentals=0),
        name="forward",
    )(hbm(freq_rows), hbm(freq_cols), hbm(m), hbm(g))


def momentum_left(both, coeffs, row, high, low):
    rows, cols = both.shape[0] // 2, both.shape[1]
    n = len(spans(cols))
    return pl.pallas_call(
        momentum_kernel,
        out_shape=[jax.ShapeDtypeStruct((rows, cols), jnp.bfloat16), pltpu.VMEM((rows, 48), jnp.bfloat16)],
        in_specs=[VMEM] * 5,
        out_specs=[ANY, VMEM],
        scratch_shapes=[pltpu.VMEM((rows, cols), jnp.bfloat16), pltpu.SemaphoreType.DMA((len(spans(cols)),))],
        compiler_params=PARAMS,
        cost_estimate=pl.CostEstimate(flops=2 * 48 * rows * cols, bytes_accessed=2 * rows * cols, transcendentals=0),
        name="momentum",
    )(both, coeffs, row, high, low)


def updated(core, total, squares, row, high, low, cols, entries, before=None):
    rows = row.shape[0]
    given = [total, squares, row, high, low] + ([] if before is None else [before])
    return pl.pallas_call(
        functools.partial(update_kernel, entries, core),
        out_shape=jax.ShapeDtypeStruct((rows, cols), jnp.float32),
        in_specs=[VMEM] * 5 + [ANY] * (len(given) - 5),
        out_specs=ANY,
        input_output_aliases={} if before is None else {5: 0},
        scratch_shapes=[pltpu.VMEM((rows, cols), jnp.float32), pltpu.SemaphoreType.DMA((len(WRITES),))],
        compiler_params=PARAMS,
        cost_estimate=pl.CostEstimate(flops=2 * 48 * rows * cols, bytes_accessed=4 * rows * cols, transcendentals=0),
        name="update",
    )(*given)


def moved(v, partner):
    pairs = []
    for d in range(256):
        z, y, x, near, core = d // 32, d // 8 % 4, d // 4 % 2, d // 2 % 2, d % 2
        z, y, x, near, core = partner(z, y, x, near, core)
        pairs.append((d, (((z * 4 + y) * 2 + x) * 2 + near) * 2 + core))
    return lax.ppermute(v, ("rep", "tp"), pairs)


def replica(dz, dy, dx):
    def partner(z, y, x, near, core):
        if core == 0:
            return (z ^ 1, y, x, near, core) if dy else (z, y ^ 1, x, near, core)
        return z ^ dz, y ^ dy, x ^ dx, near, core

    return partner


def other_core(z, y, x, near, core):
    return z, y, x, near, 1 - core


def next_chip(z, y, x, near, core):
    return z, y, x, 1 - near, core


def four_way(v, a, b):
    both = tuple(i ^ j for i, j in zip(a, b))
    return (v + moved(v, replica(*a))) + (moved(v, replica(*b)) + moved(v, replica(*both)))


def body(momentum, grad, freq_rows, freq_cols):
    m, g = momentum[0], grad[0]
    rows, cols = m.shape
    tp = lax.axis_size("tp")
    own, row, high, low, both = forward(freq_rows, freq_cols, m, g)
    count = own.shape[0]
    other = moved(own, other_core)
    pair = jnp.concatenate([other, own], axis=0)
    pair = four_way(pair, (0, 1, 0), (0, 2, 0))
    pair = four_way(pair, (1, 0, 0), (3, 0, 0))
    kept, turned = momentum_left(both, own, row, high, low)
    other, kept, turned = lax.optimization_barrier((moved(pair, replica(6, 0, 0)), kept, turned))
    pair = pair + other
    pair = pair + moved(pair, replica(0, 0, 1))
    squares = pair * pair
    squares = sum(squares[k : k + KEEP] for k in range(0, 2 * count, KEEP))
    squares = squares + moved(squares, next_chip)
    entries = float(rows * cols * tp)
    sent = moved(jnp.concatenate([pair[:count], squares], axis=0), other_core)
    update = updated(1, pair[count:], squares, turned, high, low, cols, entries)
    update = updated(0, sent[:count], sent[count:], turned, high, low, cols, entries, update)
    return kept[None], update


def solution(mesh):
    placed = (P("rep", None, "tp"), P("rep", None, "tp"), P(), P())
    return jax.shard_map(
        body,
        mesh=mesh,
        in_specs=placed,
        out_specs=(P("rep", None, "tp"), P(None, "tp")),
        check_vma=False,
    )
```

```python
import functools
import math

import jax
import jax.numpy as jnp
from jax import lax
from jax.experimental import pallas as pl
from jax.experimental.pallas import tpu as pltpu
from jax.sharding import PartitionSpec as P

BLOCK = 64
KEEP = 8
LANES = 128
SPAN = 1024
VMEM_BYTES = 16 * 1024 * 1024
TILES = SPAN // LANES
WRITES = [(0, 512), (512, 1024), (1536, 1920)]
READS = [(0, 1536), (1536, 1920)]


def spans(cols):
    return [(start, min(SPAN, cols - start)) for start in range(0, cols, SPAN)]


def basis_tiles(fr_ref, fc_ref):
    row = lax.broadcasted_iota(jnp.int32, (2 * KEEP, LANES), 0)
    point = lax.broadcasted_iota(jnp.int32, (2 * KEEP, LANES), 1) & (BLOCK - 1)
    freq = jnp.zeros((2 * KEEP, LANES), jnp.int32)
    for k in range(KEEP):
        freq = jnp.where(row == k, fr_ref[k], freq)
        freq = jnp.where(row == KEEP + k, fc_ref[k], freq)
    turn = ((2 * point + 1) * freq) & (4 * BLOCK - 1)
    turn = jnp.minimum(turn, 4 * BLOCK - turn)
    x = (BLOCK - turn).astype(jnp.float32) * (math.pi / (2 * BLOCK))
    y = x * x
    series = jnp.full_like(x, 1.0 / math.factorial(13))
    for n in (11, 9, 7, 5, 3, 1):
        series = 1.0 / math.factorial(n) - series * y
    scale = jnp.where(freq == 0, math.sqrt(1.0 / BLOCK), math.sqrt(2.0 / BLOCK))
    return x * series * scale


def split(v):
    high = v.astype(jnp.bfloat16)
    return high, (v - high.astype(jnp.float32)).astype(jnp.bfloat16)


def two_blocks(tile):
    lane = lax.broadcasted_iota(jnp.int32, (KEEP, LANES), 1)
    return jnp.concatenate([jnp.where(lane < BLOCK, tile, 0.0), jnp.where(lane >= BLOCK, tile, 0.0)], axis=0)


def only(t, v):
    lane = lax.broadcasted_iota(jnp.int32, v.shape, 1)
    return jnp.where((lane >> 4) == t, v, 0.0)


def dot(a, b, dims):
    return lax.dot_general(a, b, (dims, ((), ())), preferred_element_type=jnp.float32)


def packed_rows(cols):
    whole, left = divmod(cols, SPAN)
    assert 0 < left <= SPAN // 2
    return 16 * whole + 8


def pack(spans16):
    last = spans16[-1]
    return jnp.concatenate(spans16[:-1] + [last[:8] + pltpu.roll(last[8:], LANES // 2, 1)], axis=0)


def unpack(rows):
    last = rows[-8:]
    return jnp.concatenate([rows, pltpu.roll(last, LANES // 2, 1)], axis=0)


def forward_kernel(
    fr_ref, fc_ref, m_ref, g_ref, out_ref, row_ref, high_ref, low_ref, both, fr_smem, fc_smem, fsems, sems
):
    cols = m_ref.shape[1]
    freqs = [
        pltpu.make_async_copy(src, dst, fsems.at[k]) for k, (src, dst) in enumerate(((fr_ref, fr_smem), (fc_ref, fc_smem)))
    ]
    for copy in freqs:
        copy.start()
    copies = []
    for n, (start, width) in enumerate(READS):
        for k, src in enumerate((m_ref, g_ref)):
            copy = pltpu.make_async_copy(
                src.at[:, pl.ds(start, width)], both.at[pl.ds(LANES * k, LANES), pl.ds(start, width)], sems.at[n, k]
            )
            copy.start()
            copies.append(copy)
    for copy in freqs:
        copy.wait()
    tiles = basis_tiles(fr_smem, fc_smem)
    rows = two_blocks(tiles[:KEEP])
    row_ref[...] = rows
    high, low = split(jnp.concatenate([0.9 * rows, rows], axis=1))
    lhs = jnp.concatenate([high, low], axis=0)
    high, low = split(two_blocks(tiles[KEEP:]))
    high_ref[...] = jnp.concatenate([high] * TILES, axis=0)
    low_ref[...] = jnp.concatenate([low] * TILES, axis=0)
    high_tiles, low_tiles = [], []
    for n, (start, width) in enumerate(READS):
        copies[2 * n].wait()
        copies[2 * n + 1].wait()
        y = dot(lhs, both[:, start : start + width], ((1,), (0,)))
        high, low = split(y[:16] + y[16:])
        high_tiles += [high[:, k : k + LANES] for k in range(0, width, LANES)]
        low_tiles += [low[:, k : k + LANES] for k in range(0, width, LANES)]
    y_high = jnp.concatenate(high_tiles, axis=0)
    y_both = jnp.concatenate([y_high, jnp.concatenate(low_tiles, axis=0)], axis=1)
    c = dot(y_both, jnp.concatenate([high_ref[...]] * 2, axis=1), ((1,), (1,)))
    c = c + dot(y_high, low_ref[...], ((1,), (1,)))
    sums = []
    for first in range(0, cols // LANES, TILES):
        parts = [only(t - first, c[16 * t : 16 * t + 16]) for t in range(first, min(first + TILES, cols // LANES))]
        while len(parts) > 1:
            parts = [sum(parts[k : k + 2]) for k in range(0, len(parts), 2)]
        sums.append(parts[0])
    out_ref[...] = pack(sums)


def half_image(c, high_ref, low_ref, tiles):
    high = c.astype(jnp.bfloat16).astype(jnp.float32)
    low = c - high

    def spread(v):
        return jnp.concatenate(
            [only(t % TILES, v[t // TILES * 16 : t // TILES * 16 + 16]).astype(jnp.bfloat16) for t in tiles], axis=0
        )

    high = spread(high)
    count = high.shape[0]
    z = dot(jnp.concatenate([high, spread(low)], axis=0), high_ref[...], ((1,), (0,)))
    z = z[:count] + z[count:] + dot(high, low_ref[...], ((1,), (0,)))
    z_high, z_low = split(z)
    return jnp.concatenate(
        [jnp.concatenate([z_high[k : k + 16], z_low[k : k + 16], z_high[k : k + 16]], axis=0) for k in range(0, count, 16)],
        axis=1,
    )


def momentum_kernel(both, c_ref, row_ref, high_ref, low_ref, out_ref, turned_ref, held, sems):
    high, low = split(jnp.transpose(jnp.concatenate([row_ref[...]] * 3, axis=0)))
    third = lax.broadcasted_iota(jnp.int32, high.shape, 1) >= 32
    rows = jnp.where(third, low.astype(jnp.float32), high.astype(jnp.float32)).astype(jnp.bfloat16)
    turned_ref[...] = rows
    halves = half_image(unpack(c_ref[...]), high_ref, low_ref, range(out_ref.shape[1] // LANES))
    copies = []
    for n, (start, width) in enumerate(spans(out_ref.shape[1])):
        here = slice(start, start + width)
        image = dot(rows, halves[:, here], ((1,), (0,)))
        fresh = 0.9 * both[:LANES, here].astype(jnp.float32) + both[LANES:, here].astype(jnp.float32)
        held[:, here] = (fresh - image).astype(jnp.bfloat16)
        copy = pltpu.make_async_copy(held.at[:, pl.ds(start, width)], out_ref.at[:, pl.ds(start, width)], sems.at[n])
        copy.start()
        copies.append(copy)
    for copy in copies:
        copy.wait()


def update_kernel(entries, core, total_ref, squares_ref, row_ref, high_ref, low_ref, *refs):
    out_ref, held, sems = refs[-3:]

    @pl.when(lax.axis_index("tp") % 2 == core)
    def _():
        rows = row_ref[...]
        c = unpack(total_ref[...])
        squares = jnp.sum(squares_ref[...])
        scale = lax.rsqrt(jnp.full((LANES, LANES), squares, jnp.float32) * (1.0 / entries) + 1e-06)
        first = WRITES[0][1]
        halves = [
            half_image(c, high_ref, low_ref, range(first // LANES)),
            half_image(c, high_ref, low_ref, range(first // LANES, out_ref.shape[1] // LANES)),
        ]
        copies = []
        for n, (start, width) in enumerate(WRITES):
            here = slice(start, start + width)
            half = halves[0] if n == 0 else halves[1][:, start - first : start - first + width]
            image = dot(rows, half, ((1,), (0,)))
            held[:, here] = image * jnp.concatenate([scale] * (width // LANES), axis=1)
            copy = pltpu.make_async_copy(held.at[:, pl.ds(start, width)], out_ref.at[:, pl.ds(start, width)], sems.at[n])
            copy.start()
            copies.append(copy)
        for copy in copies:
            copy.wait()


VMEM = pl.BlockSpec(memory_space=pltpu.VMEM)
ANY = pl.BlockSpec(memory_space=pl.ANY)
PARAMS = pltpu.CompilerParams(vmem_limit_bytes=VMEM_BYTES)


def hbm(x):
    return pltpu.with_memory_space_constraint(x, pltpu.HBM)


def forward(freq_rows, freq_cols, m, g):
    rows, cols = m.shape
    return pl.pallas_call(
        forward_kernel,
        out_shape=[
            jax.ShapeDtypeStruct((packed_rows(cols), LANES), jnp.float32),
            pltpu.VMEM((16, LANES), jnp.float32),
            pltpu.VMEM((LANES, LANES), jnp.bfloat16),
            pltpu.VMEM((LANES, LANES), jnp.bfloat16),
            pltpu.VMEM((2 * rows, cols), jnp.bfloat16),
        ],
        in_specs=[ANY] * 4,
        out_specs=[VMEM] * 5,
        scratch_shapes=[
            pltpu.SMEM((KEEP,), jnp.int32),
            pltpu.SMEM((KEEP,), jnp.int32),
            pltpu.SemaphoreType.DMA((2,)),
            pltpu.SemaphoreType.DMA((len(READS), 2)),
        ],
        compiler_params=PARAMS,
        cost_estimate=pl.CostEstimate(flops=2 * 48 * rows * cols, bytes_accessed=4 * rows * cols, transcendentals=0),
        name="forward",
    )(hbm(freq_rows), hbm(freq_cols), hbm(m), hbm(g))


def momentum_left(both, coeffs, row, high, low):
    rows, cols = both.shape[0] // 2, both.shape[1]
    n = len(spans(cols))
    return pl.pallas_call(
        momentum_kernel,
        out_shape=[jax.ShapeDtypeStruct((rows, cols), jnp.bfloat16), pltpu.VMEM((rows, 48), jnp.bfloat16)],
        in_specs=[VMEM] * 5,
        out_specs=[ANY, VMEM],
        scratch_shapes=[pltpu.VMEM((rows, cols), jnp.bfloat16), pltpu.SemaphoreType.DMA((len(spans(cols)),))],
        compiler_params=PARAMS,
        cost_estimate=pl.CostEstimate(flops=2 * 48 * rows * cols, bytes_accessed=2 * rows * cols, transcendentals=0),
        name="momentum",
    )(both, coeffs, row, high, low)


def updated(core, total, squares, row, high, low, cols, entries, before=None):
    rows = row.shape[0]
    given = [total, squares, row, high, low] + ([] if before is None else [before])
    return pl.pallas_call(
        functools.partial(update_kernel, entries, core),
        out_shape=jax.ShapeDtypeStruct((rows, cols), jnp.float32),
        in_specs=[VMEM] * 5 + [ANY] * (len(given) - 5),
        out_specs=ANY,
        input_output_aliases={} if before is None else {5: 0},
        scratch_shapes=[pltpu.VMEM((rows, cols), jnp.float32), pltpu.SemaphoreType.DMA((len(WRITES),))],
        compiler_params=PARAMS,
        cost_estimate=pl.CostEstimate(flops=2 * 48 * rows * cols, bytes_accessed=4 * rows * cols, transcendentals=0),
        name="update",
    )(*given)


def moved(v, partner):
    pairs = []
    for d in range(256):
        z, y, x, near, core = d // 32, d // 8 % 4, d // 4 % 2, d // 2 % 2, d % 2
        z, y, x, near, core = partner(z, y, x, near, core)
        pairs.append((d, (((z * 4 + y) * 2 + x) * 2 + near) * 2 + core))
    return lax.ppermute(v, ("rep", "tp"), pairs)


def replica(dz, dy, dx):
    def partner(z, y, x, near, core):
        if core == 0:
            return (z, y ^ 1, x, near, core) if dx else (z, y, x, 1 - near, core)
        return z ^ dz, y ^ dy, x ^ dx, near, core

    return partner


def other_core(z, y, x, near, core):
    return z, y, x, near, 1 - core


def next_chip(z, y, x, near, core):
    return z, y, x, 1 - near, core


def four_way(v, a, b):
    both = tuple(i ^ j for i, j in zip(a, b))
    return (v + moved(v, replica(*a))) + (moved(v, replica(*b)) + moved(v, replica(*both)))


def body(momentum, grad, freq_rows, freq_cols):
    m, g = momentum[0], grad[0]
    rows, cols = m.shape
    tp = lax.axis_size("tp")
    own, row, high, low, both = forward(freq_rows, freq_cols, m, g)
    count = own.shape[0]
    other = moved(own, other_core)
    pair = jnp.concatenate([other, own], axis=0)
    pair = four_way(pair, (0, 1, 0), (0, 2, 0))
    pair = four_way(pair, (1, 0, 0), (3, 0, 0))
    kept, turned = momentum_left(both, own, row, high, low)
    other, kept, turned = lax.optimization_barrier((moved(pair, replica(6, 0, 0)), kept, turned))
    pair = pair + other
    pair = pair + moved(pair, replica(0, 0, 1))
    squares = pair * pair
    squares = sum(squares[k : k + KEEP] for k in range(0, 2 * count, KEEP))
    squares = squares + moved(squares, next_chip)
    entries = float(rows * cols * tp)
    sent = moved(jnp.concatenate([pair[:count], squares], axis=0), other_core)
    update = updated(1, pair[count:], squares, turned, high, low, cols, entries)
    update = updated(0, sent[:count], sent[count:], turned, high, low, cols, entries, update)
    return kept[None], update


def solution(mesh):
    placed = (P("rep", None, "tp"), P("rep", None, "tp"), P(), P())
    return jax.shard_map(
        body,
        mesh=mesh,
        in_specs=placed,
        out_specs=(P("rep", None, "tp"), P(None, "tp")),
        check_vma=False,
    )
```
